128 devices in a mesh: row: 8 (over x, y_lo), col: 16 (over z, y_hi, core).
Axes of the slice: x: 4, y: 4 (y_hi: 2, y_lo: 2; y = y_hi * 2 + y_lo), z: 4, core: 2. Of those that a mesh axis runs over, the one named last changes fastest.
Arguments:
- x_slab: bfloat16 [16, 32, 64, 128], P('row', 'col'), may hold values from -220 to 220
- h_blocks: bfloat16 [16, 32, 25, 4096], P('row', 'col'), may hold values from -0.21875 to 0.21875
- h_cols: int32 [16, 32, 25], P('row', 'col'), may hold values from 0 to 511, as said below
- h_count: int32 [16, 32], P('row', 'col'), may hold values from 1 to 25, as said below
- z_blocks: bfloat16 [16, 32, 25, 4096], P('row', 'col'), may hold values from -0.15625 to 0.15625
- z_cols: int32 [16, 32, 25], P('row', 'col'), may hold values from 0 to 511, as said below
- z_count: int32 [16, 32], P('row', 'col'), may hold values from 1 to 25, as said below
Outputs:
- cheb_one: bfloat16 [16, 32, 64, 128], P('row', 'col')
- cheb_two: bfloat16 [16, 32, 64, 128], P('row', 'col')
The draws below stay inside these ranges and needn't reach their ends.
Inputs may be any that keep to these rules, and one draw needn't show every extreme that they name: `h_cols`: the 25 entries of a block cell name the 25 distinct cells within 2 cells of it along each lattice dimension, the lattice being periodic; only the first h_count entries of a cell are live, the others are padding. `h_count`: some cell has 25 live entries and some cell has 1. `z_cols`: the 25 entries of a block cell name the 25 distinct cells within 2 cells of it along each lattice dimension, the lattice being periodic; only the first z_count entries of a cell are live, the others are padding. `z_count`: some cell has 25 live entries and some cell has 1.
All inputs are finite; a program needn't handle non-finite values.
Results may differ from the reference program's by a relative error of at most 0.0085.
Values may be sent and summed in bfloat16 or wider, within the bound.
No kernel may reach another device: no remote copies, remote signals or barrier semaphores. Data moves between devices by JAX's collectives and lax.ppermute only.
A program may use at most 64 MiB of HBM per device.

```python
import jax
import jax.numpy as jnp
from jax import lax

BLOCK = 64
SIDE = 2
SLAB = 128
REACH = 2
ENTRIES = 25
LAT_Y = 16
LAT_X = 32


def draw_x_slab(key, part):
    noise_key, row_key, col_key = jax.random.split(key, 3)
    values = jax.random.truncated_normal(noise_key, -4.0, 4.0, (LAT_Y, LAT_X, BLOCK, SLAB), jnp.float32)
    row_scale = jnp.exp(jax.random.uniform(row_key, (LAT_Y, LAT_X, BLOCK, 1), jnp.float32, -1.15, 1.15))
    col_scale = jnp.exp(jax.random.uniform(col_key, (1, 1, 1, SLAB), jnp.float32, -1.15, 1.15))
    lat_row = lax.broadcasted_iota(jnp.int32, (LAT_Y, LAT_X, 1, 1), 0)
    lat_col = lax.broadcasted_iota(jnp.int32, (LAT_Y, LAT_X, 1, 1), 1)
    domain_id = lat_row // SIDE * (LAT_X // SIDE) + lat_col // SIDE
    domain_total = LAT_Y // SIDE * (LAT_X // SIDE)
    position = domain_id.astype(jnp.float32) / max(domain_total - 1, 1)
    trend_scale = jnp.sqrt(1.0 + 2.0 * position)
    return (values * row_scale * col_scale * trend_scale).astype(jnp.bfloat16)


def entry_lists(key, salt):
    base_key = jax.random.fold_in(key, salt)
    cap_key, fill_key, full_key, spot_key, least_key, order_key = jax.random.split(base_key, 6)
    domain_total = LAT_Y // SIDE * (LAT_X // SIDE)
    domain_ids = jnp.arange(domain_total, dtype=jnp.int32)
    full_domain = jax.random.randint(full_key, (), 0, domain_total)
    domain_caps = jax.random.randint(cap_key, (domain_total,), ENTRIES // 3, ENTRIES + 1)
    domain_caps = jnp.where(domain_ids == full_domain, ENTRIES, domain_caps)
    lat_row = lax.broadcasted_iota(jnp.int32, (LAT_Y, LAT_X), 0)
    lat_col = lax.broadcasted_iota(jnp.int32, (LAT_Y, LAT_X), 1)
    domain_of = lat_row // SIDE * (LAT_X // SIDE) + lat_col // SIDE
    local_cell = lat_row % SIDE * SIDE + lat_col % SIDE
    cell_cap = domain_caps[domain_of]
    counts = jax.random.randint(fill_key, (LAT_Y, LAT_X), jnp.maximum(cell_cap // 2, 1), cell_cap + 1)
    spot_cells = jax.random.randint(spot_key, (domain_total,), 0, SIDE * SIDE)
    counts = jnp.where(local_cell == spot_cells[domain_of], cell_cap, counts)
    least_domain = (full_domain + 1 + jax.random.randint(least_key, (), 0, max(domain_total - 1, 1))) % domain_total
    least_spot = (domain_of == least_domain) & (local_cell == (spot_cells[domain_of] + 1) % (SIDE * SIDE))
    counts = jnp.where(least_spot, 1, counts)
    cell_keys = jax.random.split(order_key, LAT_Y * LAT_X)
    orders = jax.vmap(lambda one_key: jax.random.permutation(one_key, ENTRIES))(cell_keys)
    orders = orders.reshape(LAT_Y, LAT_X, ENTRIES).astype(jnp.int32)
    stencil_side = 2 * REACH + 1
    shift_y = orders // stencil_side - REACH
    shift_x = orders % stencil_side - REACH
    near_row = (lat_row[:, :, None] + shift_y) % LAT_Y
    near_col = (lat_col[:, :, None] + shift_x) % LAT_X
    cell_ids = near_row * LAT_X + near_col
    return (cell_ids.astype(jnp.int32), counts.astype(jnp.int32))


def draw_h_cols(key, part):
    return entry_lists(key, 11)[0]


def draw_h_count(key, part):
    return entry_lists(key, 11)[1]


def draw_z_cols(key, part):
    return entry_lists(key, 29)[0]


def draw_z_count(key, part):
    return entry_lists(key, 29)[1]


def steps_of(key, extent, shards, smallest, top_value):
    factor_of = 1.0
    for dim, parts in shards:
        draws = jax.random.uniform(jax.random.fold_in(jax.random.fold_in(key, 6), dim), (parts,), jnp.float32, smallest / len(shards), top_value / len(shards))
        factor_of = factor_of * jnp.repeat(jnp.exp(draws), extent[dim] // parts).reshape((-1,) + (1,) * (len(extent) - 1 - dim))
    return factor_of


def gaussian(own_key, extent, deviation, most, cuts=(), held_as=jnp.bfloat16):
    result = deviation * jax.random.normal(own_key, extent, jnp.float32)
    if cuts:
        result = result * steps_of(own_key, extent, cuts, -0.22, 0.18)
    return jnp.clip(result, -most, most).astype(held_as)


def setup_inputs(seed: int = 0) -> dict:
    key_list = jax.random.split(jax.random.key(seed), 8)
    return {
        "x_slab": draw_x_slab(jax.random.fold_in(key_list[7], 71), 0),
        "h_blocks": gaussian(key_list[1], (LAT_Y, LAT_X, ENTRIES, BLOCK * BLOCK), (ENTRIES * BLOCK // 2) ** -0.5, 0.21875, ((0, 8), (1, 16))),
        "h_cols": draw_h_cols(jax.random.fold_in(key_list[7], 71), 0),
        "h_count": draw_h_count(jax.random.fold_in(key_list[7], 71), 0),
        "z_blocks": gaussian(key_list[4], (LAT_Y, LAT_X, ENTRIES, BLOCK * BLOCK), (ENTRIES * BLOCK) ** -0.5, 0.15625, ((0, 8), (1, 16))),
        "z_cols": draw_z_cols(jax.random.fold_in(key_list[7], 71), 0),
        "z_count": draw_z_count(jax.random.fold_in(key_list[7], 71), 0),
    }


def apply_sparse(slab_field, blocks, col_ids, live_count):
    grid_rows, grid_cols, block_size, slab_cols = slab_field.shape
    max_entries = col_ids.shape[2]
    flat_grid = slab_field.reshape(grid_rows * grid_cols, block_size, slab_cols).astype(jnp.float32)
    is_live = (jnp.arange(max_entries, dtype=jnp.int32)[None, None, :] < live_count[:, :, None]).astype(jnp.float32)

    def one_row(packed):
        row_blocks, row_cols, row_live = packed
        picked = flat_grid[row_cols.astype(jnp.int32)] * row_live[:, :, None, None]
        block_mats = row_blocks.astype(jnp.float32).reshape(grid_cols, max_entries, block_size, block_size)
        return jnp.einsum('xkij,xkjs->xis', block_mats, picked)
    return lax.map(one_row, (blocks, col_ids, is_live))

def reference(x_slab, h_blocks, h_cols, h_count, z_blocks, z_cols, z_count):

    def apply_root(slab_field):
        return slab_field.astype(jnp.float32) + apply_sparse(slab_field, z_blocks, z_cols, z_count)

    def apply_hamilton(slab_field):
        return apply_sparse(slab_field, h_blocks, h_cols, h_count).astype(jnp.bfloat16)
    u_one = apply_root(x_slab).astype(jnp.bfloat16)
    u_two = apply_hamilton(u_one)
    power_image = apply_root(u_two)
    slab_float = x_slab.astype(jnp.float32)
    scale_ratio = jnp.sqrt(jnp.sum(power_image * power_image) / (jnp.sum(slab_float * slab_float) + 1e-06))
    cheb_one = (power_image / scale_ratio).astype(jnp.bfloat16)
    v_one = apply_root(cheb_one).astype(jnp.bfloat16)
    v_two = apply_hamilton(v_one)
    v_three = apply_root(v_two)
    cheb_two = (2.0 * v_three / scale_ratio - slab_float).astype(jnp.bfloat16)
    return (cheb_one, cheb_two)
```

```python
import functools

import jax
import jax.numpy as jnp
from jax import lax
from jax.experimental import pallas as pl
from jax.experimental.pallas import tpu as pltpu
from jax.sharding import PartitionSpec as P

REACH = 2
SIDE = 2
BLOCK = 64
SLAB = 128
ENTRIES = 25
LAT_Y = 16
LAT_X = 32
CELLS = SIDE * SIDE
HALF = BLOCK // 2
WIDE = SIDE + 2 * REACH
THIRD = WIDE * SIDE * BLOCK
DEPTH = 3 * THIRD
ROWS = CELLS * BLOCK


def vmem():
    return pl.BlockSpec(memory_space=pltpu.VMEM)


def smem():
    return pl.BlockSpec(memory_space=pltpu.SMEM)


def build_kernel(origin_ref, cols_ref, count_ref, blocks_ref, out_ref, wide_ref):
    out_ref[...] = jnp.zeros_like(out_ref)
    wide_ref[...] = blocks_ref[...].astype(jnp.float32)
    lane_half = lax.broadcasted_iota(jnp.int32, (HALF, 2 * BLOCK), 1) // BLOCK
    for cell_y in range(SIDE):
        for cell_x in range(SIDE):
            cell = cell_y * SIDE + cell_x

            def place(entry, carry, cell_y=cell_y, cell_x=cell_x, cell=cell):
                col_id = cols_ref[cell_y, cell_x, entry]
                step_y = lax.rem(lax.div(col_id, LAT_X) - origin_ref[0] - cell_y + REACH + LAT_Y, LAT_Y)
                step_x = lax.rem(lax.rem(col_id, LAT_X) - origin_ref[1] - cell_x + REACH + LAT_X, LAT_X)
                win_y = step_y + cell_y
                win_x = step_x + cell_x
                tile = lax.div(win_x, 2) * WIDE + win_y
                side = lax.rem(win_x, 2)
                base = pl.multiple_of((cell_y * ENTRIES + entry) * BLOCK, BLOCK)
                pair = wide_ref[pl.ds(base + cell_x, HALF, stride=2), :]
                turned = pltpu.roll(pair, BLOCK, 1)
                here = lane_half == side
                lanes = pl.ds(pl.multiple_of(tile * 2 * BLOCK, 2 * BLOCK), 2 * BLOCK)
                for parity in range(2):
                    first = parity * CELLS * HALF + cell * HALF
                    rows = pl.ds(first, HALF)
                    new = jnp.where(side == parity, pair, turned)
                    old = out_ref[rows, lanes].astype(jnp.float32)
                    out_ref[rows, lanes] = jnp.where(here, new, old).astype(jnp.bfloat16)
                return carry

            lax.fori_loop(0, count_ref[cell_y, cell_x], place, 0)


def build(origin, blocks, cols, count):
    rows = blocks.reshape(SIDE, SIDE, ENTRIES, HALF, 2 * BLOCK).transpose(0, 2, 3, 1, 4)
    rows = rows.reshape(SIDE * ENTRIES * HALF * SIDE, 2 * BLOCK)
    return pl.pallas_call(
        build_kernel,
        out_shape=jax.ShapeDtypeStruct((ROWS, DEPTH), jnp.bfloat16),
        in_specs=[smem(), smem(), smem(), vmem()],
        out_specs=vmem(),
        scratch_shapes=[pltpu.VMEM(rows.shape, jnp.float32)],
        compiler_params=pltpu.CompilerParams(vmem_limit_bytes=24 * 2**20),
        cost_estimate=pl.CostEstimate(flops=10_000_000, bytes_accessed=4_000_000, transcendentals=0),
    )(origin, cols, count, rows)


def product(mat_ref, left_ref, mid_ref, right_ref, turn_ref):
    total = jnp.dot(mat_ref[:, :THIRD], left_ref[...], preferred_element_type=jnp.float32)
    total += jnp.dot(mat_ref[:, THIRD : 2 * THIRD], mid_ref[...], preferred_element_type=jnp.float32)
    total += jnp.dot(mat_ref[:, 2 * THIRD :], right_ref[...], preferred_element_type=jnp.float32)
    for cell in range(CELLS):
        for parity in range(2):
            first = parity * CELLS * HALF + cell * HALF
            turn_ref[pl.ds(cell * BLOCK + parity, HALF, stride=2), :] = total[first : first + HALF]
    return turn_ref[...]


def root_kernel(mat_ref, left_ref, mid_ref, right_ref, own_ref, out_ref, turn_ref):
    image = product(mat_ref, left_ref, mid_ref, right_ref, turn_ref)
    out_ref[...] = (own_ref[...].astype(jnp.float32) + image).astype(jnp.bfloat16)


def hamilton_kernel(mat_ref, left_ref, mid_ref, right_ref, out_ref, turn_ref):
    out_ref[...] = product(mat_ref, left_ref, mid_ref, right_ref, turn_ref).astype(jnp.bfloat16)


def power_kernel(mat_ref, left_ref, mid_ref, right_ref, own_ref, slab_ref, out_ref, power_ref, sums_ref, turn_ref):
    power = own_ref[...].astype(jnp.float32) + product(mat_ref, left_ref, mid_ref, right_ref, turn_ref)
    slab = slab_ref[...].astype(jnp.float32)
    power_ref[...] = power
    out_ref[...] = power.astype(jnp.bfloat16)
    image_square = jnp.sum(power * power)
    slab_square = jnp.sum(slab * slab)
    row = lax.broadcasted_iota(jnp.int32, sums_ref.shape, 0)
    sums_ref[...] = jnp.where(row == 0, image_square, slab_square)


def last_kernel(mat_ref, left_ref, mid_ref, right_ref, own_ref, slab_ref, power_ref, sums_ref, one_ref, two_ref, turn_ref):
    sums = sums_ref[...]
    ratio = jnp.sqrt(sums[0:1] / (sums[1:2] + 1e-06))
    image = own_ref[...].astype(jnp.float32) + product(mat_ref, left_ref, mid_ref, right_ref, turn_ref)
    one_ref[...] = (power_ref[...] / ratio).astype(jnp.bfloat16)
    two_ref[...] = (2.0 * (image / ratio) / ratio - slab_ref[...].astype(jnp.float32)).astype(jnp.bfloat16)


def apply(kernel, outs, *operands):
    return pl.pallas_call(
        kernel,
        out_shape=outs,
        in_specs=[vmem()] * len(operands),
        out_specs=jax.tree.map(lambda _: vmem(), outs),
        scratch_shapes=[pltpu.VMEM((ROWS, SLAB), jnp.float32)],
        compiler_params=pltpu.CompilerParams(vmem_limit_bytes=16 * 2**20),
        cost_estimate=pl.CostEstimate(flops=2 * ROWS * DEPTH * SLAB, bytes_accessed=2_000_000, transcendentals=0),
    )(*operands)


def around(value, axis):
    count = lax.axis_size(axis)
    before = lax.ppermute(value, axis, [(i, (i + 1) % count) for i in range(count)])
    after = lax.ppermute(value, axis, [((i + 1) % count, i) for i in range(count)])
    return before, after


def surround(field):
    above, below = around(field, "row")
    mid = jnp.concatenate([above, field, below], axis=0)
    left, right = around(mid, "col")
    return left, mid, right


def total_of(sums):
    for axis in ("row", "col"):
        count = lax.axis_size(axis)
        bit = 1
        while bit < count:
            sums = sums + lax.ppermute(sums, axis, [(i, i ^ bit) for i in range(count)])
            bit *= 2
    return sums


def body(x_slab, h_blocks, h_cols, h_count, z_blocks, z_cols, z_count):
    origin = jnp.stack([lax.axis_index("row") * SIDE, lax.axis_index("col") * SIDE]).astype(jnp.int32)
    z_mat = build(origin, z_blocks, z_cols, z_count)
    h_mat = build(origin, h_blocks, h_cols, h_count)
    flat = jax.ShapeDtypeStruct((ROWS, SLAB), jnp.bfloat16)
    wide = jax.ShapeDtypeStruct((ROWS, SLAB), jnp.float32)
    sums_shape = jax.ShapeDtypeStruct((8, SLAB), jnp.float32)
    slab = x_slab.reshape(ROWS, SLAB)

    u_one = apply(root_kernel, flat, z_mat, *surround(slab), slab)
    u_two = apply(hamilton_kernel, flat, h_mat, *surround(u_one))
    power, power_full, sums = apply(power_kernel, (flat, wide, sums_shape), z_mat, *surround(u_two), u_two, slab)
    v_one = apply(root_kernel, flat, z_mat, *surround(power), power)
    v_two = apply(hamilton_kernel, flat, h_mat, *surround(v_one))
    sums = total_of(sums)
    one, two = apply(last_kernel, (flat, flat), z_mat, *surround(v_two), v_two, slab, power_full, sums)
    return one.reshape(x_slab.shape), two.reshape(x_slab.shape)


def solution(mesh):
    in_specs = (
        P("row", "col", None, None),
        P("row", "col", None, None),
        P("row", "col", None),
        P("row", "col"),
        P("row", "col", None, None),
        P("row", "col", None),
        P("row", "col"),
    )
    out_specs = (P("row", "col", None, None), P("row", "col", None, None))
    return jax.shard_map(body, mesh=mesh, in_specs=in_specs, out_specs=out_specs, check_vma=False)
```

```python
import jax
import jax.numpy as jnp
from jax import lax
from jax.experimental import pallas as pl
from jax.experimental.pallas import tpu as pltpu
from jax.sharding import PartitionSpec as P

REACH = 2
SIDE = 2
BLOCK = 64
SLAB = 128
ENTRIES = 25
LAT_Y = 16
LAT_X = 32
CELLS = SIDE * SIDE
HALF = BLOCK // 2
LANES = 2 * BLOCK
ROWS = CELLS * BLOCK
PARTS = 9
DEPTH = PARTS * ROWS
BLOCK_ROWS = CELLS * ENTRIES * HALF


def vmem():
    return pl.BlockSpec(memory_space=pltpu.VMEM)


def smem():
    return pl.BlockSpec(memory_space=pltpu.SMEM)


def role(step, is_odd):
    return jnp.where(step == 1, 0, jnp.where((step == 2) == (is_odd == 0), 1, 2))


def build_kernel(origin_ref, cols_any, count_any, blocks_any, out_ref, blocks_ref, wide_ref, cols_ref, count_ref, sems):
    copies = [
        pltpu.make_async_copy(blocks_any, blocks_ref, sems.at[0]),
        pltpu.make_async_copy(cols_any, cols_ref, sems.at[1]),
        pltpu.make_async_copy(count_any, count_ref, sems.at[2]),
    ]
    for copy in copies:
        copy.start()
    out_ref[...] = jnp.zeros_like(out_ref)
    for copy in copies:
        copy.wait()
    wide_ref[...] = blocks_ref[...].astype(jnp.float32)
    lane_half = lax.broadcasted_iota(jnp.int32, (HALF, LANES), 1) // BLOCK
    odd_y = origin_ref[0] % 2
    odd_x = origin_ref[1] % 2

    def place(entry, carry):
        loaded = []
        for cell in range(CELLS):
            cell_y, cell_x = divmod(cell, SIDE)
            col_id = cols_ref[cell_y, cell_x, entry]
            step_y = (lax.div(col_id, LAT_X) - origin_ref[0] * SIDE - cell_y + REACH) & (LAT_Y - 1)
            step_x = (lax.rem(col_id, LAT_X) - origin_ref[1] * SIDE - cell_x + REACH) & (LAT_X - 1)
            win_y = step_y + cell_y
            win_x = step_x + cell_x
            part = role(win_x >> 1, odd_x) * 3 + role(win_y >> 1, odd_y)
            tile = jnp.where(entry < count_ref[cell_y, cell_x], part * 2 + (win_y & 1), 2 * PARTS)
            side = win_x & 1
            base = pl.multiple_of((cell_y * ENTRIES + entry) * BLOCK, BLOCK)
            pair = wide_ref[pl.ds(base + cell_x, HALF, stride=2), :]
            lanes = pl.ds(pl.multiple_of(tile * LANES, LANES), LANES)
            spots = [(pl.ds(parity * CELLS * HALF + cell * HALF, HALF), lanes) for parity in range(2)]
            olds = [out_ref[spot].astype(jnp.float32) for spot in spots]
            loaded.append((side, pair, spots, olds))
        stores = []
        for side, pair, spots, olds in loaded:
            turned = pltpu.roll(pair, BLOCK, 1)
            here = lane_half == side
            for parity in range(2):
                new = jnp.where(side == parity, pair, turned)
                stores.append((spots[parity], jnp.where(here, new, olds[parity]).astype(jnp.bfloat16)))
        for spot, value in stores:
            out_ref[spot] = value
        return carry

    counts = [count_ref[divmod(cell, SIDE)] for cell in range(CELLS)]
    most = jnp.maximum(jnp.maximum(counts[0], counts[1]), jnp.maximum(counts[2], counts[3]))
    lax.fori_loop(0, most, place, 0)


def build(origin, blocks, cols, count):
    rows = blocks.reshape(SIDE, SIDE, ENTRIES, HALF, LANES).transpose(0, 2, 3, 1, 4).reshape(BLOCK_ROWS, LANES)
    any_space = pl.BlockSpec(memory_space=pl.ANY)
    return pl.pallas_call(
        build_kernel,
        out_shape=jax.ShapeDtypeStruct((ROWS, DEPTH + LANES), jnp.bfloat16),
        in_specs=[smem(), any_space, any_space, any_space],
        out_specs=vmem(),
        scratch_shapes=[
            pltpu.VMEM(rows.shape, jnp.bfloat16),
            pltpu.VMEM(rows.shape, jnp.float32),
            pltpu.SMEM(cols.shape, jnp.int32),
            pltpu.SMEM(count.shape, jnp.int32),
            pltpu.SemaphoreType.DMA((3,)),
        ],
        compiler_params=pltpu.CompilerParams(vmem_limit_bytes=16 * 2**20),
        cost_estimate=pl.CostEstimate(flops=10_000_000, bytes_accessed=4_000_000, transcendentals=0),
    )(origin, cols, count, rows)


def product(mat_ref, part_refs, turn_ref):
    total = None
    for index, part_ref in enumerate(part_refs):
        term = jnp.dot(mat_ref[:, index * ROWS : (index + 1) * ROWS], part_ref[...], preferred_element_type=jnp.float32)
        total = term if total is None else total + term
    for cell in range(CELLS):
        for parity in range(2):
            first = parity * CELLS * HALF + cell * HALF
            turn_ref[pl.ds(cell * BLOCK + parity, HALF, stride=2), :] = total[first : first + HALF]
    return turn_ref[...]


def root_kernel(mat_ref, *refs):
    *part_refs, out_ref, turn_ref = refs
    own = part_refs[0][...].astype(jnp.float32)
    out_ref[...] = (own + product(mat_ref, part_refs, turn_ref)).astype(jnp.bfloat16)


def hamilton_kernel(mat_ref, *refs):
    *part_refs, out_ref, turn_ref = refs
    out_ref[...] = product(mat_ref, part_refs, turn_ref).astype(jnp.bfloat16)


def power_kernel(mat_ref, slab_ref, *refs):
    *part_refs, out_ref, power_ref, sums_ref, turn_ref = refs
    power = part_refs[0][...].astype(jnp.float32) + product(mat_ref, part_refs, turn_ref)
    slab = slab_ref[...].astype(jnp.float32)
    power_ref[...] = power
    out_ref[...] = power.astype(jnp.bfloat16)
    image_square = jnp.sum(power * power)
    slab_square = jnp.sum(slab * slab)
    row = lax.broadcasted_iota(jnp.int32, sums_ref.shape, 0)
    sums_ref[...] = jnp.where(row == 0, image_square, slab_square)


def last_kernel(mat_ref, slab_ref, power_ref, sums_ref, *refs):
    *part_refs, one_ref, two_ref, turn_ref = refs
    sums = sums_ref[...]
    ratio = jnp.sqrt(sums[0:1] / (sums[1:2] + 1e-06))
    image = part_refs[0][...].astype(jnp.float32) + product(mat_ref, part_refs, turn_ref)
    one_ref[...] = (power_ref[...] / ratio).astype(jnp.bfloat16)
    two_ref[...] = (2.0 * (image / ratio) / ratio - slab_ref[...].astype(jnp.float32)).astype(jnp.bfloat16)


def apply(kernel, outs, *operands):
    return pl.pallas_call(
        kernel,
        out_shape=outs,
        in_specs=[vmem()] * len(operands),
        out_specs=jax.tree.map(lambda _: vmem(), outs),
        scratch_shapes=[pltpu.VMEM((ROWS, SLAB), jnp.float32)],
        compiler_params=pltpu.CompilerParams(vmem_limit_bytes=16 * 2**20),
        cost_estimate=pl.CostEstimate(flops=2 * ROWS * DEPTH * SLAB, bytes_accessed=2_000_000, transcendentals=0),
    )(*operands)


def same(index, count):
    return index


def near(index, count):
    return index ^ 1


def cross(index, count):
    return (index + 1 if index % 2 else index - 1) % count


def swap(value, row_map, col_map):
    rows, cols = lax.axis_size("row"), lax.axis_size("col")
    pairs = [(r * cols + c, row_map(r, rows) * cols + col_map(c, cols)) for r in range(rows) for c in range(cols)]
    return lax.ppermute(value, ("row", "col"), pairs)


def surround(field):
    near_y = swap(field, near, same)
    far_y = swap(field, cross, same)
    across = [swap(field, row_map, cross) for row_map in (same, near, cross)]
    beside = swap(field, same, near)
    near_y, far_y, *across = lax.optimization_barrier((near_y, far_y, *across))
    beside_near = swap(near_y, same, near)
    beside_far = swap(far_y, same, near)
    return [field, near_y, far_y, beside, beside_near, beside_far, *across]


def total_of(sums, axis, bits):
    count = lax.axis_size(axis)
    for bit in bits:
        sums = sums + lax.ppermute(sums, axis, [(i, i ^ bit) for i in range(count)])
    return sums


def body(x_slab, h_blocks, h_cols, h_count, z_blocks, z_cols, z_count):
    origin = jnp.stack([lax.axis_index("row"), lax.axis_index("col")]).astype(jnp.int32)
    z_mat = build(origin, z_blocks, z_cols, z_count)
    h_mat = build(origin, h_blocks, h_cols, h_count)
    flat = jax.ShapeDtypeStruct((ROWS, SLAB), jnp.bfloat16)
    wide = jax.ShapeDtypeStruct((ROWS, SLAB), jnp.float32)
    sums_shape = jax.ShapeDtypeStruct((8, SLAB), jnp.float32)
    slab = x_slab.reshape(ROWS, SLAB)

    u_one = apply(root_kernel, flat, z_mat, *surround(slab))
    u_two = apply(hamilton_kernel, flat, h_mat, *surround(u_one))
    power, power_full, sums = apply(power_kernel, (flat, wide, sums_shape), z_mat, slab, *surround(u_two))

    parts = surround(power)
    sums = total_of(sums, "col", (1,))
    sums = total_of(sums, "row", (1, 2))
    sums, *parts = lax.optimization_barrier((sums, *parts))
    v_one = apply(root_kernel, flat, z_mat, *parts)

    parts = surround(v_one)
    sums = total_of(sums, "col", (4, 2))
    sums, *parts = lax.optimization_barrier((sums, *parts))
    v_two = apply(hamilton_kernel, flat, h_mat, *parts)

    parts = surround(v_two)
    sums = total_of(sums, "row", (4,))
    sums = total_of(sums, "col", (8,))
    one, two = apply(last_kernel, (flat, flat), z_mat, slab, power_full, sums, *parts)
    return one.reshape(x_slab.shape), two.reshape(x_slab.shape)


def solution(mesh):
    in_specs = (
        P("row", "col", None, None),
        P("row", "col", None, None),
        P("row", "col", None),
        P("row", "col"),
        P("row", "col", None, None),
        P("row", "col", None),
        P("row", "col"),
    )
    out_specs = (P("row", "col", None, None), P("row", "col", None, None))
    return jax.shard_map(body, mesh=mesh, in_specs=in_specs, out_specs=out_specs, check_vma=False)
```

```python
import jax
import jax.numpy as jnp
from jax import lax
from jax.experimental import pallas as pl
from jax.experimental.pallas import tpu as pltpu
from jax.sharding import PartitionSpec as P

REACH = 2
SIDE = 2
BLOCK = 64
SLAB = 128
ENTRIES = 25
LAT_Y = 16
LAT_X = 32
CELLS = SIDE * SIDE
HALF = BLOCK // 2
LANES = 2 * BLOCK
ROWS = CELLS * BLOCK
PARTS = 9
DEPTH = PARTS * ROWS
BLOCK_ROWS = CELLS * ENTRIES * HALF


def vmem():
    return pl.BlockSpec(memory_space=pltpu.VMEM)


def smem():
    return pl.BlockSpec(memory_space=pltpu.SMEM)


def role(step, is_odd):
    return jnp.where(step == 1, 0, jnp.where((step == 2) == (is_odd == 0), 1, 2))


def build_kernel(origin_ref, cols_any, count_any, blocks_any, out_ref, blocks_ref, wide_ref, cols_ref, count_ref, sems):
    copies = [
        pltpu.make_async_copy(blocks_any, blocks_ref, sems.at[0]),
        pltpu.make_async_copy(cols_any, cols_ref, sems.at[1]),
        pltpu.make_async_copy(count_any, count_ref, sems.at[2]),
    ]
    for copy in copies:
        copy.start()
    out_ref[...] = jnp.zeros_like(out_ref)
    for copy in copies:
        copy.wait()
    wide_ref[...] = blocks_ref[...].astype(jnp.float32)
    lane_half = lax.broadcasted_iota(jnp.int32, (HALF, LANES), 1) // BLOCK
    odd_y = origin_ref[0] % 2
    odd_x = origin_ref[1] % 2

    def place(entry, carry):
        loaded = []
        for cell in range(CELLS):
            cell_y, cell_x = divmod(cell, SIDE)
            col_id = cols_ref[cell_y, cell_x, entry]
            step_y = (lax.div(col_id, LAT_X) - origin_ref[0] * SIDE - cell_y + REACH) & (LAT_Y - 1)
            step_x = (lax.rem(col_id, LAT_X) - origin_ref[1] * SIDE - cell_x + REACH) & (LAT_X - 1)
            win_y = step_y + cell_y
            win_x = step_x + cell_x
            part = role(win_x >> 1, odd_x) * 3 + role(win_y >> 1, odd_y)
            tile = jnp.where(entry < count_ref[cell_y, cell_x], part * 2 + (win_y & 1), 2 * PARTS)
            side = win_x & 1
            base = pl.multiple_of((cell_y * ENTRIES + entry) * BLOCK, BLOCK)
            pair = wide_ref[pl.ds(base + cell_x, HALF, stride=2), :]
            lanes = pl.ds(pl.multiple_of(tile * LANES, LANES), LANES)
            spots = [(pl.ds(parity * CELLS * HALF + cell * HALF, HALF), lanes) for parity in range(2)]
            olds = [out_ref[spot].astype(jnp.float32) for spot in spots]
            loaded.append((side, pair, spots, olds))
        stores = []
        for side, pair, spots, olds in loaded:
            turned = pltpu.roll(pair, BLOCK, 1)
            here = lane_half == side
            for parity in range(2):
                new = jnp.where(side == parity, pair, turned)
                stores.append((spots[parity], jnp.where(here, new, olds[parity]).astype(jnp.bfloat16)))
        for spot, value in stores:
            out_ref[spot] = value
        return carry

    counts = [count_ref[divmod(cell, SIDE)] for cell in range(CELLS)]
    most = jnp.maximum(jnp.maximum(counts[0], counts[1]), jnp.maximum(counts[2], counts[3]))
    lax.fori_loop(0, most, place, 0)


def build(origin, blocks, cols, count):
    rows = blocks.reshape(SIDE, SIDE, ENTRIES, HALF, LANES).transpose(0, 2, 3, 1, 4).reshape(BLOCK_ROWS, LANES)
    any_space = pl.BlockSpec(memory_space=pltpu.HBM)
    return pl.pallas_call(
        build_kernel,
        out_shape=jax.ShapeDtypeStruct((ROWS, DEPTH + LANES), jnp.bfloat16),
        in_specs=[smem(), any_space, any_space, any_space],
        out_specs=vmem(),
        scratch_shapes=[
            pltpu.VMEM(rows.shape, jnp.bfloat16),
            pltpu.VMEM(rows.shape, jnp.float32),
            pltpu.SMEM(cols.shape, jnp.int32),
            pltpu.SMEM(count.shape, jnp.int32),
            pltpu.SemaphoreType.DMA((3,)),
        ],
        compiler_params=pltpu.CompilerParams(vmem_limit_bytes=16 * 2**20),
        cost_estimate=pl.CostEstimate(flops=10_000_000, bytes_accessed=4_000_000, transcendentals=0),
    )(origin, cols, count, rows)


def product(mat_ref, part_refs, turn_ref):
    total = None
    for index, part_ref in enumerate(part_refs):
        term = jnp.dot(mat_ref[:, index * ROWS : (index + 1) * ROWS], part_ref[...], preferred_element_type=jnp.float32)
        total = term if total is None else total + term
    for cell in range(CELLS):
        for parity in range(2):
            first = parity * CELLS * HALF + cell * HALF
            turn_ref[pl.ds(cell * BLOCK + parity, HALF, stride=2), :] = total[first : first + HALF]
    return turn_ref[...]


def root_kernel(mat_ref, *refs):
    *part_refs, out_ref, turn_ref = refs
    own = part_refs[0][...].astype(jnp.float32)
    out_ref[...] = (own + product(mat_ref, part_refs, turn_ref)).astype(jnp.bfloat16)


def hamilton_kernel(mat_ref, *refs):
    *part_refs, out_ref, turn_ref = refs
    out_ref[...] = product(mat_ref, part_refs, turn_ref).astype(jnp.bfloat16)


def power_kernel(mat_ref, slab_ref, *refs):
    *part_refs, out_ref, power_ref, sums_ref, turn_ref = refs
    power = part_refs[0][...].astype(jnp.float32) + product(mat_ref, part_refs, turn_ref)
    slab = slab_ref[...].astype(jnp.float32)
    power_ref[...] = power
    out_ref[...] = power.astype(jnp.bfloat16)
    image_square = jnp.sum(power * power)
    slab_square = jnp.sum(slab * slab)
    row = lax.broadcasted_iota(jnp.int32, sums_ref.shape, 0)
    sums_ref[...] = jnp.where(row == 0, image_square, slab_square)


def last_kernel(mat_ref, slab_ref, power_ref, sums_ref, *refs):
    *part_refs, one_ref, two_ref, turn_ref = refs
    sums = sums_ref[...]
    ratio = jnp.sqrt(sums[0:1] / (sums[1:2] + 1e-06))
    image = part_refs[0][...].astype(jnp.float32) + product(mat_ref, part_refs, turn_ref)
    one_ref[...] = (power_ref[...] / ratio).astype(jnp.bfloat16)
    two_ref[...] = (2.0 * (image / ratio) / ratio - slab_ref[...].astype(jnp.float32)).astype(jnp.bfloat16)


def apply(kernel, outs, *operands):
    return pl.pallas_call(
        kernel,
        out_shape=outs,
        in_specs=[vmem()] * len(operands),
        out_specs=jax.tree.map(lambda _: vmem(), outs),
        scratch_shapes=[pltpu.VMEM((ROWS, SLAB), jnp.float32)],
        compiler_params=pltpu.CompilerParams(vmem_limit_bytes=16 * 2**20),
        cost_estimate=pl.CostEstimate(flops=2 * ROWS * DEPTH * SLAB, bytes_accessed=2_000_000, transcendentals=0),
    )(*operands)


def same(index, count):
    return index


def near(index, count):
    return index ^ 1


def cross(index, count):
    return (index + 1 if index % 2 else index - 1) % count


def swap(value, row_map, col_map):
    rows, cols = lax.axis_size("row"), lax.axis_size("col")
    pairs = [(r * cols + c, row_map(r, rows) * cols + col_map(c, cols)) for r in range(rows) for c in range(cols)]
    return lax.ppermute(value, ("row", "col"), pairs)


def surround(field, early=(), late=()):
    near_y = swap(field, near, same)
    far_y = swap(field, cross, same)
    across_far = swap(field, cross, cross)
    across_same = swap(field, same, cross)
    across_near = swap(field, near, cross)
    beside = swap(field, same, near)
    *late, across_near, across_same, across_far, far_y, near_y = lax.optimization_barrier(
        (*late, across_near, across_same, across_far, far_y, near_y, *early)
    )[: len(late) + 5]
    beside_near = swap(near_y, same, near)
    beside_far = swap(far_y, same, near)
    return [field, near_y, far_y, beside, beside_near, beside_far, across_same, across_near, across_far], late


def total_of(sums, axis, bit):
    count = lax.axis_size(axis)
    return sums + lax.ppermute(sums, axis, [(i, i ^ bit) for i in range(count)])


def body(x_slab, h_blocks, h_cols, h_count, z_blocks, z_cols, z_count):
    origin = jnp.stack([lax.axis_index("row"), lax.axis_index("col")]).astype(jnp.int32)
    z_mat = build(origin, z_blocks, z_cols, z_count)
    h_mat = build(origin, h_blocks, h_cols, h_count)
    flat = jax.ShapeDtypeStruct((ROWS, SLAB), jnp.bfloat16)
    wide = jax.ShapeDtypeStruct((ROWS, SLAB), jnp.float32)
    sums_shape = jax.ShapeDtypeStruct((8, SLAB), jnp.float32)
    slab = x_slab.reshape(ROWS, SLAB)

    parts, (z_mat,) = surround(slab, late=(z_mat,))
    u_one = apply(root_kernel, flat, z_mat, *parts)
    parts, (h_mat,) = surround(u_one, late=(h_mat,))
    u_two = apply(hamilton_kernel, flat, h_mat, *parts)
    parts, _ = surround(u_two)
    power, power_full, sums = apply(power_kernel, (flat, wide, sums_shape), z_mat, slab, *parts)

    first = total_of(sums, "row", 1)
    parts, (sums,) = surround(power, early=(first,), late=(total_of(first, "row", 4),))
    v_one = apply(root_kernel, flat, z_mat, *parts)

    first = total_of(sums, "row", 2)
    parts, (sums,) = surround(v_one, early=(first,), late=(total_of(first, "col", 2),))
    v_two = apply(hamilton_kernel, flat, h_mat, *parts)

    first = total_of(sums, "col", 4)
    parts, (sums,) = surround(v_two, early=(first,), late=(total_of(first, "col", 8),))
    sums = total_of(sums, "col", 1)
    one, two = apply(last_kernel, (flat, flat), z_mat, slab, power_full, sums, *parts)
    return one.reshape(x_slab.shape), two.reshape(x_slab.shape)


def solution(mesh):
    in_specs = (
        P("row", "col", None, None),
        P("row", "col", None, None),
        P("row", "col", None),
        P("row", "col"),
        P("row", "col", None, None),
        P("row", "col", None),
        P("row", "col"),
    )
    out_specs = (P("row", "col", None, None), P("row", "col", None, None))
    return jax.shard_map(body, mesh=mesh, in_specs=in_specs, out_specs=out_specs, check_vma=False)
```

```python
import jax
import jax.numpy as jnp
from jax import lax
from jax.experimental import pallas as pl
from jax.experimental.pallas import tpu as pltpu
from jax.sharding import PartitionSpec as P

REACH = 2
SIDE = 2
BLOCK = 64
SLAB = 128
ENTRIES = 25
LAT_Y = 16
LAT_X = 32
CELLS = SIDE * SIDE
HALF = BLOCK // 2
LANES = 2 * BLOCK
ROWS = CELLS * BLOCK
PARTS = 9
DEPTH = PARTS * ROWS
BLOCK_ROWS = CELLS * ENTRIES * HALF


def vmem():
    return pl.BlockSpec(memory_space=pltpu.VMEM)


def smem():
    return pl.BlockSpec(memory_space=pltpu.SMEM)


def role(step, is_odd):
    return jnp.where(step == 1, 0, jnp.where((step == 2) == (is_odd == 0), 1, 2))


def build_kernel(origin_ref, cols_any, count_any, blocks_any, out_ref, blocks_ref, wide_ref, cols_ref, count_ref, sems):
    copies = [
        pltpu.make_async_copy(blocks_any, blocks_ref, sems.at[0]),
        pltpu.make_async_copy(cols_any, cols_ref, sems.at[1]),
        pltpu.make_async_copy(count_any, count_ref, sems.at[2]),
    ]
    for copy in copies:
        copy.start()
    out_ref[...] = jnp.zeros_like(out_ref)
    for copy in copies:
        copy.wait()
    wide_ref[...] = blocks_ref[...].astype(jnp.float32)
    lane_half = lax.broadcasted_iota(jnp.int32, (HALF, LANES), 1) // BLOCK
    odd_y = origin_ref[0] % 2
    odd_x = origin_ref[1] % 2

    def place(entry, carry):
        loaded = []
        for cell in range(CELLS):
            cell_y, cell_x = divmod(cell, SIDE)
            col_id = cols_ref[cell_y, cell_x, entry]
            step_y = (lax.div(col_id, LAT_X) - origin_ref[0] * SIDE - cell_y + REACH) & (LAT_Y - 1)
            step_x = (lax.rem(col_id, LAT_X) - origin_ref[1] * SIDE - cell_x + REACH) & (LAT_X - 1)
            win_y = step_y + cell_y
            win_x = step_x + cell_x
            part = role(win_x >> 1, odd_x) * 3 + role(win_y >> 1, odd_y)
            tile = jnp.where(entry < count_ref[cell_y, cell_x], part * 2 + (win_y & 1), 2 * PARTS)
            side = win_x & 1
            base = pl.multiple_of((cell_y * ENTRIES + entry) * BLOCK, BLOCK)
            pair = wide_ref[pl.ds(base + cell_x, HALF, stride=2), :]
            lanes = pl.ds(pl.multiple_of(tile * LANES, LANES), LANES)
            spots = [(pl.ds(parity * CELLS * HALF + cell * HALF, HALF), lanes) for parity in range(2)]
            olds = [out_ref[spot].astype(jnp.float32) for spot in spots]
            loaded.append((side, pair, spots, olds))
        stores = []
        for side, pair, spots, olds in loaded:
            turned = pltpu.roll(pair, BLOCK, 1)
            here = lane_half == side
            for parity in range(2):
                new = jnp.where(side == parity, pair, turned)
                stores.append((spots[parity], jnp.where(here, new, olds[parity]).astype(jnp.bfloat16)))
        for spot, value in stores:
            out_ref[spot] = value
        return carry

    counts = [count_ref[divmod(cell, SIDE)] for cell in range(CELLS)]
    most = jnp.maximum(jnp.maximum(counts[0], counts[1]), jnp.maximum(counts[2], counts[3]))
    lax.fori_loop(0, most, place, 0)


def build(origin, blocks, cols, count):
    rows = blocks.reshape(SIDE, SIDE, ENTRIES, HALF, LANES).transpose(0, 2, 3, 1, 4).reshape(BLOCK_ROWS, LANES)
    any_space = pl.BlockSpec(memory_space=pltpu.HBM)
    return pl.pallas_call(
        build_kernel,
        out_shape=jax.ShapeDtypeStruct((ROWS, DEPTH + LANES), jnp.bfloat16),
        in_specs=[smem(), any_space, any_space, any_space],
        out_specs=vmem(),
        scratch_shapes=[
            pltpu.VMEM(rows.shape, jnp.bfloat16),
            pltpu.VMEM(rows.shape, jnp.float32),
            pltpu.SMEM(cols.shape, jnp.int32),
            pltpu.SMEM(count.shape, jnp.int32),
            pltpu.SemaphoreType.DMA((3,)),
        ],
        compiler_params=pltpu.CompilerParams(vmem_limit_bytes=16 * 2**20),
        cost_estimate=pl.CostEstimate(flops=10_000_000, bytes_accessed=4_000_000, transcendentals=0),
    )(origin, cols, count, rows)


def product(mat_ref, part_refs, turn_ref):
    total = None
    for index, part_ref in enumerate(part_refs):
        term = jnp.dot(mat_ref[:, index * ROWS : (index + 1) * ROWS], part_ref[...], preferred_element_type=jnp.float32)
        total = term if total is None else total + term
    for cell in range(CELLS):
        for parity in range(2):
            first = parity * CELLS * HALF + cell * HALF
            turn_ref[pl.ds(cell * BLOCK + parity, HALF, stride=2), :] = total[first : first + HALF]
    return turn_ref[...]


def root_kernel(mat_ref, *refs):
    *part_refs, out_ref, turn_ref = refs
    own = part_refs[0][...].astype(jnp.float32)
    out_ref[...] = (own + product(mat_ref, part_refs, turn_ref)).astype(jnp.bfloat16)


def hamilton_kernel(mat_ref, *refs):
    *part_refs, out_ref, turn_ref = refs
    out_ref[...] = product(mat_ref, part_refs, turn_ref).astype(jnp.bfloat16)


def root_sums_kernel(mat_ref, term_ref, other_ref, *refs):
    *part_refs, out_ref, sums_ref, turn_ref = refs
    sums_ref[...] = term_ref[...] + other_ref[...]
    root_kernel(mat_ref, *part_refs, out_ref, turn_ref)


def hamilton_sums_kernel(mat_ref, term_ref, other_ref, *refs):
    *part_refs, out_ref, sums_ref, turn_ref = refs
    sums_ref[...] = term_ref[...] + other_ref[...]
    hamilton_kernel(mat_ref, *part_refs, out_ref, turn_ref)


def power_kernel(mat_ref, slab_ref, *refs):
    *part_refs, out_ref, power_ref, sums_ref, turn_ref = refs
    power = part_refs[0][...].astype(jnp.float32) + product(mat_ref, part_refs, turn_ref)
    slab = slab_ref[...].astype(jnp.float32)
    power_ref[...] = power
    out_ref[...] = power.astype(jnp.bfloat16)
    image_square = jnp.sum(power * power)
    slab_square = jnp.sum(slab * slab)
    row = lax.broadcasted_iota(jnp.int32, sums_ref.shape, 0)
    sums_ref[...] = jnp.where(row == 0, image_square, slab_square)


def last_kernel(mat_ref, slab_ref, power_ref, sums_ref, *refs):
    *part_refs, one_ref, two_ref, turn_ref = refs
    sums = sums_ref[...]
    ratio = jnp.sqrt(sums[0:1] / (sums[1:2] + 1e-06))
    image = part_refs[0][...].astype(jnp.float32) + product(mat_ref, part_refs, turn_ref)
    one_ref[...] = (power_ref[...] / ratio).astype(jnp.bfloat16)
    two_ref[...] = (2.0 * (image / ratio) / ratio - slab_ref[...].astype(jnp.float32)).astype(jnp.bfloat16)


def apply(kernel, outs, *operands):
    return pl.pallas_call(
        kernel,
        out_shape=outs,
        in_specs=[vmem()] * len(operands),
        out_specs=jax.tree.map(lambda _: vmem(), outs),
        scratch_shapes=[pltpu.VMEM((ROWS, SLAB), jnp.float32)],
        compiler_params=pltpu.CompilerParams(vmem_limit_bytes=16 * 2**20),
        cost_estimate=pl.CostEstimate(flops=2 * ROWS * DEPTH * SLAB, bytes_accessed=2_000_000, transcendentals=0),
    )(*operands)


def same(index, count):
    return index


def near(index, count):
    return index ^ 1


def cross(index, count):
    return (index + 1 if index % 2 else index - 1) % count


def swap(value, row_map, col_map):
    rows, cols = lax.axis_size("row"), lax.axis_size("col")
    pairs = [(r * cols + c, row_map(r, rows) * cols + col_map(c, cols)) for r in range(rows) for c in range(cols)]
    return lax.ppermute(value, ("row", "col"), pairs)


def surround(field, late=(), whole=True):
    near_y = swap(field, near, same)
    far_y = swap(field, cross, same)
    across_far = swap(field, cross, cross)
    across_same = swap(field, same, cross)
    across_near = swap(field, near, cross)
    beside = swap(field, same, near)
    if whole:
        *late, across_near, across_same, across_far, far_y, near_y = lax.optimization_barrier(
            (*late, across_near, across_same, across_far, far_y, near_y)
        )
    else:
        across_near, far_y, near_y = lax.optimization_barrier((across_near, far_y, near_y))
    beside_near = swap(near_y, same, near)
    beside_far = swap(far_y, same, near)
    return [field, near_y, far_y, beside, beside_near, beside_far, across_same, across_near, across_far], late


def flipped(sums, axis, bit):
    count = lax.axis_size(axis)
    return lax.ppermute(sums, axis, [(i, i ^ bit) for i in range(count)])


def body(x_slab, h_blocks, h_cols, h_count, z_blocks, z_cols, z_count):
    origin = jnp.stack([lax.axis_index("row"), lax.axis_index("col")]).astype(jnp.int32)
    z_mat = build(origin, z_blocks, z_cols, z_count)
    h_mat = build(origin, h_blocks, h_cols, h_count)
    flat = jax.ShapeDtypeStruct((ROWS, SLAB), jnp.bfloat16)
    wide = jax.ShapeDtypeStruct((ROWS, SLAB), jnp.float32)
    sums_shape = jax.ShapeDtypeStruct((8, SLAB), jnp.float32)
    slab = x_slab.reshape(ROWS, SLAB)

    parts, (z_mat,) = surround(slab, late=(z_mat,))
    u_one = apply(root_kernel, flat, z_mat, *parts)
    parts, (h_mat,) = surround(u_one, late=(h_mat,))
    u_two = apply(hamilton_kernel, flat, h_mat, *parts)
    parts, _ = surround(u_two, whole=False)
    power, power_full, sums = apply(power_kernel, (flat, wide, sums_shape), z_mat, slab, *parts)

    pair = sums + flipped(sums, "row", 4)
    other = flipped(pair, "row", 1)
    parts, (pair,) = surround(power, late=(pair,))
    v_one, sums = apply(root_sums_kernel, (flat, sums_shape), z_mat, pair, other, *parts)

    pair = sums + flipped(sums, "col", 2)
    other = flipped(pair, "row", 2)
    parts, (pair,) = surround(v_one, late=(pair,))
    v_two, sums = apply(hamilton_sums_kernel, (flat, sums_shape), h_mat, pair, other, *parts)

    pair = sums + flipped(sums, "col", 8)
    other = flipped(pair, "col", 4)
    parts, (pair,) = surround(v_two, late=(pair,))
    sums = pair + other
    sums = sums + flipped(sums, "col", 1)
    one, two = apply(last_kernel, (flat, flat), z_mat, slab, power_full, sums, *parts)
    return one.reshape(x_slab.shape), two.reshape(x_slab.shape)


def solution(mesh):
    in_specs = (
        P("row", "col", None, None),
        P("row", "col", None, None),
        P("row", "col", None),
        P("row", "col"),
        P("row", "col", None, None),
        P("row", "col", None),
        P("row", "col"),
    )
    out_specs = (P("row", "col", None, None), P("row", "col", None, None))
    return jax.shard_map(body, mesh=mesh, in_specs=in_specs, out_specs=out_specs, check_vma=False)
```

```python
import jax
import jax.numpy as jnp
from jax import lax
from jax.experimental import pallas as pl
from jax.experimental.pallas import tpu as pltpu
from jax.sharding import PartitionSpec as P

REACH = 2
SIDE = 2
BLOCK = 64
SLAB = 128
ENTRIES = 25
LAT_Y = 16
LAT_X = 32
CELLS = SIDE * SIDE
HALF = BLOCK // 2
LANES = 2 * BLOCK
ROWS = CELLS * BLOCK
PARTS = 9
DEPTH = PARTS * ROWS
NOTE = 16
BLOCK_ROWS = CELLS * ENTRIES * HALF


def vmem():
    return pl.BlockSpec(memory_space=pltpu.VMEM)


def smem():
    return pl.BlockSpec(memory_space=pltpu.SMEM)


def role(step, is_odd):
    return jnp.where(step == 1, 0, jnp.where((step == 2) == (is_odd == 0), 1, 2))


def build_kernel(origin_ref, cols_any, count_any, blocks_any, out_ref, blocks_ref, wide_ref, cols_ref, count_ref, sems):
    copies = [
        pltpu.make_async_copy(blocks_any, blocks_ref, sems.at[0]),
        pltpu.make_async_copy(cols_any, cols_ref, sems.at[1]),
        pltpu.make_async_copy(count_any, count_ref, sems.at[2]),
    ]
    for copy in copies:
        copy.start()
    out_ref[...] = jnp.zeros_like(out_ref)
    for copy in copies:
        copy.wait()
    wide_ref[...] = blocks_ref[...].astype(jnp.float32)
    lane_half = lax.broadcasted_iota(jnp.int32, (HALF, LANES), 1) // BLOCK
    odd_y = origin_ref[0] % 2
    odd_x = origin_ref[1] % 2

    def place(entry, carry):
        loaded = []
        for cell in range(CELLS):
            cell_y, cell_x = divmod(cell, SIDE)
            col_id = cols_ref[cell_y, cell_x, entry]
            step_y = (lax.div(col_id, LAT_X) - origin_ref[0] * SIDE - cell_y + REACH) & (LAT_Y - 1)
            step_x = (lax.rem(col_id, LAT_X) - origin_ref[1] * SIDE - cell_x + REACH) & (LAT_X - 1)
            win_y = step_y + cell_y
            win_x = step_x + cell_x
            part = role(win_x >> 1, odd_x) * 3 + role(win_y >> 1, odd_y)
            tile = jnp.where(entry < count_ref[cell_y, cell_x], part * 2 + (win_y & 1), 2 * PARTS)
            side = win_x & 1
            base = pl.multiple_of((cell_y * ENTRIES + entry) * BLOCK, BLOCK)
            pair = wide_ref[pl.ds(base + cell_x, HALF, stride=2), :]
            lanes = pl.ds(pl.multiple_of(tile * LANES, LANES), LANES)
            spots = [(pl.ds(parity * CELLS * HALF + cell * HALF, HALF), lanes) for parity in range(2)]
            olds = [out_ref[spot].astype(jnp.float32) for spot in spots]
            loaded.append((side, pair, spots, olds))
        stores = []
        for side, pair, spots, olds in loaded:
            turned = pltpu.roll(pair, BLOCK, 1)
            here = lane_half == side
            for parity in range(2):
                new = jnp.where(side == parity, pair, turned)
                stores.append((spots[parity], jnp.where(here, new, olds[parity]).astype(jnp.bfloat16)))
        for spot, value in stores:
            out_ref[spot] = value
        return carry

    counts = [count_ref[divmod(cell, SIDE)] for cell in range(CELLS)]
    most = jnp.maximum(jnp.maximum(counts[0], counts[1]), jnp.maximum(counts[2], counts[3]))
    lax.fori_loop(0, most, place, 0)


def build(origin, blocks, cols, count):
    rows = blocks.reshape(SIDE, SIDE, ENTRIES, HALF, LANES).transpose(0, 2, 3, 1, 4).reshape(BLOCK_ROWS, LANES)
    any_space = pl.BlockSpec(memory_space=pltpu.HBM)
    return pl.pallas_call(
        build_kernel,
        out_shape=jax.ShapeDtypeStruct((ROWS, DEPTH + LANES), jnp.bfloat16),
        in_specs=[smem(), any_space, any_space, any_space],
        out_specs=vmem(),
        scratch_shapes=[
            pltpu.VMEM(rows.shape, jnp.bfloat16),
            pltpu.VMEM(rows.shape, jnp.float32),
            pltpu.SMEM(cols.shape, jnp.int32),
            pltpu.SMEM(count.shape, jnp.int32),
            pltpu.SemaphoreType.DMA((3,)),
        ],
        compiler_params=pltpu.CompilerParams(vmem_limit_bytes=16 * 2**20),
        cost_estimate=pl.CostEstimate(flops=10_000_000, bytes_accessed=4_000_000, transcendentals=0),
    )(origin, cols, count, rows)


def product(mat_ref, part_refs, turn_ref):
    total = None
    for index, part_ref in enumerate(part_refs):
        term = jnp.dot(mat_ref[:, index * ROWS : (index + 1) * ROWS], part_ref[:ROWS], preferred_element_type=jnp.float32)
        total = term if total is None else total + term
    for cell in range(CELLS):
        for parity in range(2):
            first = parity * CELLS * HALF + cell * HALF
            turn_ref[pl.ds(cell * BLOCK + parity, HALF, stride=2), :] = total[first : first + HALF]
    return turn_ref[...]


def write_note(note, sums):
    row = lax.broadcasted_iota(jnp.int32, (NOTE, SLAB), 0)
    rest = jnp.broadcast_to(sums, (NOTE, SLAB))
    rows = jnp.zeros((NOTE, SLAB), jnp.float32)
    for index in range(3):
        term = rest.astype(jnp.bfloat16).astype(jnp.float32)
        rows = jnp.where(row == index, term, rows)
        rest = rest - term
    note[ROWS:, :] = rows.astype(jnp.bfloat16)


def read_notes(part_refs):
    notes = [jnp.sum(ref[ROWS:, :].astype(jnp.float32), axis=0, keepdims=True) for ref in part_refs]
    return notes[0] + notes[1] + notes[2] + notes[3]


def root_kernel(mat_ref, *refs):
    *part_refs, out_ref, turn_ref = refs
    own = part_refs[0][:ROWS].astype(jnp.float32)
    out_ref[...] = (own + product(mat_ref, part_refs, turn_ref)).astype(jnp.bfloat16)


def hamilton_kernel(mat_ref, *refs):
    *part_refs, out_ref, turn_ref = refs
    out_ref[...] = product(mat_ref, part_refs, turn_ref).astype(jnp.bfloat16)


def power_kernel(mat_ref, slab_ref, *refs):
    *part_refs, out_ref, power_ref, turn_ref = refs
    power = part_refs[0][...].astype(jnp.float32) + product(mat_ref, part_refs, turn_ref)
    slab = slab_ref[...].astype(jnp.float32)
    power_ref[...] = power
    out_ref[:ROWS] = power.astype(jnp.bfloat16)
    lane = lax.broadcasted_iota(jnp.int32, (1, SLAB), 1)
    write_note(out_ref, jnp.where(lane < SLAB // 2, jnp.sum(power * power), jnp.sum(slab * slab)))


def root_sums_kernel(mat_ref, *refs):
    *part_refs, out_ref, sums_ref, turn_ref = refs
    sums_ref[...] = jnp.broadcast_to(read_notes([part_refs[part] for part in (0, 1, 3, 4)]), sums_ref.shape)
    root_kernel(mat_ref, *part_refs, out_ref, turn_ref)


def hamilton_sums_kernel(mat_ref, term_ref, other_ref, *refs):
    *part_refs, out_ref, turn_ref = refs
    out_ref[:ROWS] = product(mat_ref, part_refs, turn_ref).astype(jnp.bfloat16)
    write_note(out_ref, term_ref[:1] + other_ref[:1])


def last_kernel(mat_ref, slab_ref, power_ref, *refs):
    *part_refs, one_ref, two_ref, turn_ref = refs
    sums = read_notes([part_refs[part] for part in (0, 2, 6, 8)])
    ratio = jnp.sqrt(sums[:, :1] / (sums[:, SLAB // 2 : SLAB // 2 + 1] + 1e-06))
    image = part_refs[0][:ROWS].astype(jnp.float32) + product(mat_ref, part_refs, turn_ref)
    one_ref[...] = (power_ref[...] / ratio).astype(jnp.bfloat16)
    two_ref[...] = (2.0 * (image / ratio) / ratio - slab_ref[...].astype(jnp.float32)).astype(jnp.bfloat16)


def apply(kernel, outs, *operands):
    return pl.pallas_call(
        kernel,
        out_shape=outs,
        in_specs=[vmem()] * len(operands),
        out_specs=jax.tree.map(lambda _: vmem(), outs),
        scratch_shapes=[pltpu.VMEM((ROWS, SLAB), jnp.float32)],
        compiler_params=pltpu.CompilerParams(vmem_limit_bytes=16 * 2**20),
        cost_estimate=pl.CostEstimate(flops=2 * ROWS * DEPTH * SLAB, bytes_accessed=2_000_000, transcendentals=0),
    )(*operands)


def same(index, count):
    return index


def near(index, count):
    return index ^ 1


def cross(index, count):
    return (index + 1 if index % 2 else index - 1) % count


def swap(value, row_map, col_map):
    rows, cols = lax.axis_size("row"), lax.axis_size("col")
    pairs = [(r * cols + c, row_map(r, rows) * cols + col_map(c, cols)) for r in range(rows) for c in range(cols)]
    return lax.ppermute(value, ("row", "col"), pairs)


def surround(field, late=(), whole=True):
    near_y = swap(field, near, same)
    far_y = swap(field, cross, same)
    across_far = swap(field, cross, cross)
    across_same = swap(field, same, cross)
    across_near = swap(field, near, cross)
    beside = swap(field, same, near)
    if whole:
        *late, across_near, across_same, across_far, far_y, near_y = lax.optimization_barrier(
            (*late, across_near, across_same, across_far, far_y, near_y)
        )
    else:
        across_near, far_y, near_y = lax.optimization_barrier((across_near, far_y, near_y))
    beside_near = swap(near_y, same, near)
    beside_far = swap(far_y, same, near)
    return [field, near_y, far_y, beside, beside_near, beside_far, across_same, across_near, across_far], late


def shifted(sums, axis, step):
    count = lax.axis_size(axis)
    return lax.ppermute(sums, axis, [(i, (i + step) % count) for i in range(count)])


def body(x_slab, h_blocks, h_cols, h_count, z_blocks, z_cols, z_count):
    origin = jnp.stack([lax.axis_index("row"), lax.axis_index("col")]).astype(jnp.int32)
    z_mat = build(origin, z_blocks, z_cols, z_count)
    h_mat = build(origin, h_blocks, h_cols, h_count)
    flat = jax.ShapeDtypeStruct((ROWS, SLAB), jnp.bfloat16)
    wide = jax.ShapeDtypeStruct((ROWS, SLAB), jnp.float32)
    sums_shape = jax.ShapeDtypeStruct((8, SLAB), jnp.float32)
    noted = jax.ShapeDtypeStruct((ROWS + NOTE, SLAB), jnp.bfloat16)
    slab = x_slab.reshape(ROWS, SLAB)

    parts, (z_mat,) = surround(slab, late=(z_mat,))
    u_one = apply(root_kernel, flat, z_mat, *parts)
    parts, (h_mat,) = surround(u_one, late=(h_mat,))
    u_two = apply(hamilton_kernel, flat, h_mat, *parts)
    parts, _ = surround(u_two, whole=False)
    power, power_full = apply(power_kernel, (noted, wide), z_mat, slab, *parts)

    parts, _ = surround(power, whole=False)
    v_one, sums = apply(root_sums_kernel, (flat, sums_shape), z_mat, *parts)
    ring = sums + shifted(sums, "col", 4) + shifted(sums, "col", 8) + shifted(sums, "col", 12)
    other = shifted(ring, "row", 4)
    parts, (ring,) = surround(v_one, late=(ring,))
    v_two = apply(hamilton_sums_kernel, noted, h_mat, ring, other, *parts)
    parts, _ = surround(v_two, whole=False)
    one, two = apply(last_kernel, (flat, flat), z_mat, slab, power_full, *parts)
    return one.reshape(x_slab.shape), two.reshape(x_slab.shape)


def solution(mesh):
    in_specs = (
        P("row", "col", None, None),
        P("row", "col", None, None),
        P("row", "col", None),
        P("row", "col"),
        P("row", "col", None, None),
        P("row", "col", None),
        P("row", "col"),
    )
    out_specs = (P("row", "col", None, None), P("row", "col", None, None))
    return jax.shard_map(body, mesh=mesh, in_specs=in_specs, out_specs=out_specs, check_vma=False)
```

```python
import jax
import jax.numpy as jnp
from jax import lax
from jax.experimental import pallas as pl
from jax.experimental.pallas import tpu as pltpu
from jax.sharding import PartitionSpec as P

REACH = 2
SIDE = 2
BLOCK = 64
SLAB = 128
ENTRIES = 25
LAT_Y = 16
LAT_X = 32
CELLS = SIDE * SIDE
HALF = BLOCK // 2
LANES = 2 * BLOCK
ROWS = CELLS * BLOCK
PARTS = 9
DEPTH = PARTS * ROWS
NOTE = 16
BLOCK_ROWS = CELLS * ENTRIES * HALF


def vmem():
    return pl.BlockSpec(memory_space=pltpu.VMEM)


def smem():
    return pl.BlockSpec(memory_space=pltpu.SMEM)


def role(step, is_odd):
    return jnp.where(step == 1, 0, jnp.where((step == 2) == (is_odd == 0), 1, 2))


def spots_of(cols, count):
    row, col = lax.axis_index("row"), lax.axis_index("col")
    cell_y = lax.broadcasted_iota(jnp.int32, cols.shape, 0)
    cell_x = lax.broadcasted_iota(jnp.int32, cols.shape, 1)
    win_y = (((cols >> LAT_X.bit_length() - 1) - row * SIDE - cell_y + REACH) & (LAT_Y - 1)) + cell_y
    win_x = (((cols & (LAT_X - 1)) - col * SIDE - cell_x + REACH) & (LAT_X - 1)) + cell_x
    part = role(win_x >> 1, col & 1) * 3 + role(win_y >> 1, row & 1)
    live = lax.broadcasted_iota(jnp.int32, cols.shape, 2) < count[:, :, None]
    return jnp.where(live, part * 2 + (win_y & 1), 2 * PARTS) * 2 + (win_x & 1)


def build_kernel(spots_ref, blocks_ref, out_ref, wide_ref):
    out_ref[...] = jnp.zeros_like(out_ref)
    wide_ref[...] = blocks_ref[...].astype(jnp.float32)
    lane_half = lax.broadcasted_iota(jnp.int32, (HALF, LANES), 1) // BLOCK
    low = (lane_half == 0).astype(jnp.float32).astype(jnp.bfloat16)
    high = (lane_half == 1).astype(jnp.float32).astype(jnp.bfloat16)

    def place(entry, carry):
        stores = []
        for cell in range(CELLS):
            cell_y, cell_x = divmod(cell, SIDE)
            spot = spots_ref[cell_y, cell_x, entry]
            side = spot & 1
            lanes = pl.ds(pl.multiple_of((spot >> 1) * LANES, LANES), LANES)
            base = pl.multiple_of((cell_y * ENTRIES + entry) * BLOCK, BLOCK)
            pair = wide_ref[pl.ds(base + cell_x, HALF, stride=2), :]
            mask = jnp.where(side == 0, low, high)
            for parity, value in ((side, pair), (1 - side, pltpu.roll(pair, BLOCK, 1))):
                rows = pl.ds(pl.multiple_of(parity * CELLS * HALF + cell * HALF, HALF), HALF)
                stores.append(((rows, lanes), out_ref[rows, lanes] + value.astype(jnp.bfloat16) * mask))
        for where, value in stores:
            out_ref[where] = value
        return carry

    lax.fori_loop(0, ENTRIES, place, 0, unroll=5)


def build(blocks, cols, count):
    rows = blocks.reshape(SIDE, SIDE, ENTRIES, HALF, LANES).transpose(0, 2, 3, 1, 4).reshape(BLOCK_ROWS, LANES)
    return pl.pallas_call(
        build_kernel,
        out_shape=jax.ShapeDtypeStruct((ROWS, DEPTH + LANES), jnp.bfloat16),
        in_specs=[smem(), vmem()],
        out_specs=vmem(),
        scratch_shapes=[pltpu.VMEM(rows.shape, jnp.float32)],
        compiler_params=pltpu.CompilerParams(vmem_limit_bytes=16 * 2**20),
        cost_estimate=pl.CostEstimate(flops=10_000_000, bytes_accessed=4_000_000, transcendentals=0),
    )(spots_of(cols, count), rows)


def product(mat_ref, part_refs, turn_ref):
    total = None
    for index, part_ref in enumerate(part_refs):
        term = jnp.dot(mat_ref[:, index * ROWS : (index + 1) * ROWS], part_ref[:ROWS], preferred_element_type=jnp.float32)
        total = term if total is None else total + term
    for cell in range(CELLS):
        for parity in range(2):
            first = parity * CELLS * HALF + cell * HALF
            turn_ref[pl.ds(cell * BLOCK + parity, HALF, stride=2), :] = total[first : first + HALF]
    return turn_ref[...]


def write_note(note, sums):
    row = lax.broadcasted_iota(jnp.int32, (NOTE, SLAB), 0)
    rest = jnp.broadcast_to(sums, (NOTE, SLAB))
    rows = jnp.zeros((NOTE, SLAB), jnp.float32)
    for index in range(3):
        term = rest.astype(jnp.bfloat16).astype(jnp.float32)
        rows = jnp.where(row == index, term, rows)
        rest = rest - term
    note[ROWS:, :] = rows.astype(jnp.bfloat16)


def read_notes(part_refs):
    notes = [jnp.sum(ref[ROWS:, :].astype(jnp.float32), axis=0, keepdims=True) for ref in part_refs]
    return notes[0] + notes[1] + notes[2] + notes[3]


def root_kernel(mat_ref, *refs):
    *part_refs, out_ref, turn_ref = refs
    own = part_refs[0][:ROWS].astype(jnp.float32)
    out_ref[...] = (own + product(mat_ref, part_refs, turn_ref)).astype(jnp.bfloat16)


def hamilton_kernel(mat_ref, *refs):
    *part_refs, out_ref, turn_ref = refs
    out_ref[...] = product(mat_ref, part_refs, turn_ref).astype(jnp.bfloat16)


def power_kernel(mat_ref, slab_ref, *refs):
    *part_refs, out_ref, power_ref, turn_ref = refs
    power = part_refs[0][...].astype(jnp.float32) + product(mat_ref, part_refs, turn_ref)
    slab = slab_ref[...].astype(jnp.float32)
    power_ref[...] = power
    out_ref[:ROWS] = power.astype(jnp.bfloat16)
    lane = lax.broadcasted_iota(jnp.int32, (1, SLAB), 1)
    write_note(out_ref, jnp.where(lane < SLAB // 2, jnp.sum(power * power), jnp.sum(slab * slab)))


def root_sums_kernel(mat_ref, *refs):
    *part_refs, out_ref, sums_ref, turn_ref = refs
    sums_ref[...] = jnp.broadcast_to(read_notes([part_refs[part] for part in (0, 1, 3, 4)]), sums_ref.shape)
    root_kernel(mat_ref, *part_refs, out_ref, turn_ref)


def hamilton_sums_kernel(mat_ref, term_ref, other_ref, *refs):
    *part_refs, out_ref, turn_ref = refs
    out_ref[:ROWS] = product(mat_ref, part_refs, turn_ref).astype(jnp.bfloat16)
    write_note(out_ref, term_ref[:1] + other_ref[:1])


def last_kernel(mat_ref, slab_ref, power_ref, *refs):
    *part_refs, one_ref, two_ref, turn_ref = refs
    sums = read_notes([part_refs[part] for part in (0, 2, 6, 8)])
    ratio = jnp.sqrt(sums[:, :1] / (sums[:, SLAB // 2 : SLAB // 2 + 1] + 1e-06))
    image = part_refs[0][:ROWS].astype(jnp.float32) + product(mat_ref, part_refs, turn_ref)
    one_ref[...] = (power_ref[...] / ratio).astype(jnp.bfloat16)
    two_ref[...] = (2.0 * (image / ratio) / ratio - slab_ref[...].astype(jnp.float32)).astype(jnp.bfloat16)


def apply(kernel, outs, *operands):
    return pl.pallas_call(
        kernel,
        out_shape=outs,
        in_specs=[vmem()] * len(operands),
        out_specs=jax.tree.map(lambda _: vmem(), outs),
        scratch_shapes=[pltpu.VMEM((ROWS, SLAB), jnp.float32)],
        compiler_params=pltpu.CompilerParams(vmem_limit_bytes=16 * 2**20),
        cost_estimate=pl.CostEstimate(flops=2 * ROWS * DEPTH * SLAB, bytes_accessed=2_000_000, transcendentals=0),
    )(*operands)


def same(index, count):
    return index


def near(index, count):
    return index ^ 1


def cross(index, count):
    return (index + 1 if index % 2 else index - 1) % count


def swap(value, row_map, col_map):
    rows, cols = lax.axis_size("row"), lax.axis_size("col")
    pairs = [(r * cols + c, row_map(r, rows) * cols + col_map(c, cols)) for r in range(rows) for c in range(cols)]
    return lax.ppermute(value, ("row", "col"), pairs)


def surround(field, late=(), whole=True):
    near_y = swap(field, near, same)
    far_y = swap(field, cross, same)
    across_far = swap(field, cross, cross)
    across_same = swap(field, same, cross)
    across_near = swap(field, near, cross)
    beside = swap(field, same, near)
    if whole:
        *late, across_near, across_same, across_far, far_y, near_y = lax.optimization_barrier(
            (*late, across_near, across_same, across_far, far_y, near_y)
        )
    else:
        across_near, far_y, near_y = lax.optimization_barrier((across_near, far_y, near_y))
    beside_near = swap(near_y, same, near)
    beside_far = swap(far_y, same, near)
    return [field, near_y, far_y, beside, beside_near, beside_far, across_same, across_near, across_far], late


def shifted(sums, axis, step):
    count = lax.axis_size(axis)
    return lax.ppermute(sums, axis, [(i, (i + step) % count) for i in range(count)])


def body(x_slab, h_blocks, h_cols, h_count, z_blocks, z_cols, z_count):
    z_mat = build(z_blocks, z_cols, z_count)
    h_mat = build(h_blocks, h_cols, h_count)
    flat = jax.ShapeDtypeStruct((ROWS, SLAB), jnp.bfloat16)
    wide = jax.ShapeDtypeStruct((ROWS, SLAB), jnp.float32)
    sums_shape = jax.ShapeDtypeStruct((8, SLAB), jnp.float32)
    noted = jax.ShapeDtypeStruct((ROWS + NOTE, SLAB), jnp.bfloat16)
    slab = x_slab.reshape(ROWS, SLAB)

    parts, _ = surround(slab, whole=False)
    u_one = apply(root_kernel, flat, z_mat, *parts)
    parts, _ = surround(u_one, whole=False)
    u_two = apply(hamilton_kernel, flat, h_mat, *parts)
    parts, _ = surround(u_two, whole=False)
    power, power_full = apply(power_kernel, (noted, wide), z_mat, slab, *parts)

    parts, _ = surround(power, whole=False)
    v_one, sums = apply(root_sums_kernel, (flat, sums_shape), z_mat, *parts)
    ring = sums + shifted(sums, "col", 4) + shifted(sums, "col", 8) + shifted(sums, "col", 12)
    other = shifted(ring, "row", 4)
    parts, (ring,) = surround(v_one, late=(ring,))
    v_two = apply(hamilton_sums_kernel, noted, h_mat, ring, other, *parts)
    parts, _ = surround(v_two, whole=False)
    one, two = apply(last_kernel, (flat, flat), z_mat, slab, power_full, *parts)
    return one.reshape(x_slab.shape), two.reshape(x_slab.shape)


def solution(mesh):
    in_specs = (
        P("row", "col", None, None),
        P("row", "col", None, None),
        P("row", "col", None),
        P("row", "col"),
        P("row", "col", None, None),
        P("row", "col", None),
        P("row", "col"),
    )
    out_specs = (P("row", "col", None, None), P("row", "col", None, None))
    return jax.shard_map(body, mesh=mesh, in_specs=in_specs, out_specs=out_specs, check_vma=False)
```

```python
import jax
import jax.numpy as jnp
from jax import lax
from jax.experimental import pallas as pl
from jax.experimental.pallas import tpu as pltpu
from jax.sharding import PartitionSpec as P

REACH = 2
SIDE = 2
BLOCK = 64
SLAB = 128
ENTRIES = 25
LAT_Y = 16
LAT_X = 32
CELLS = SIDE * SIDE
HALF = BLOCK // 2
LANES = 2 * BLOCK
ROWS = CELLS * BLOCK
PARTS = 9
DEPTH = PARTS * ROWS
NOTE = 16
BLOCK_ROWS = CELLS * ENTRIES * HALF


def vmem():
    return pl.BlockSpec(memory_space=pltpu.VMEM)


def smem():
    return pl.BlockSpec(memory_space=pltpu.SMEM)


def role(step, is_odd):
    return jnp.where(step == 1, 0, jnp.where((step == 2) == (is_odd == 0), 1, 2))


def spots_of(cols, count):
    row, col = lax.axis_index("row"), lax.axis_index("col")
    cell_y = lax.broadcasted_iota(jnp.int32, cols.shape, 0)
    cell_x = lax.broadcasted_iota(jnp.int32, cols.shape, 1)
    win_y = (((cols >> LAT_X.bit_length() - 1) - row * SIDE - cell_y + REACH) & (LAT_Y - 1)) + cell_y
    win_x = (((cols & (LAT_X - 1)) - col * SIDE - cell_x + REACH) & (LAT_X - 1)) + cell_x
    part = role(win_x >> 1, col & 1) * 3 + role(win_y >> 1, row & 1)
    live = lax.broadcasted_iota(jnp.int32, cols.shape, 2) < count[:, :, None]
    return jnp.where(live, part * 2 + (win_y & 1), 2 * PARTS) * 2 + (win_x & 1)


def build_kernel(spots_ref, blocks_ref, out_ref, wide_ref):
    out_ref[...] = jnp.zeros_like(out_ref)
    wide_ref[...] = blocks_ref[...].astype(jnp.float32)
    lane_half = lax.broadcasted_iota(jnp.int32, (HALF, LANES), 1) // BLOCK
    low = (lane_half == 0).astype(jnp.float32).astype(jnp.bfloat16)
    high = (lane_half == 1).astype(jnp.float32).astype(jnp.bfloat16)

    def place(entry, carry):
        stores = []
        for cell in range(CELLS):
            cell_y, cell_x = divmod(cell, SIDE)
            spot = spots_ref[cell_y, cell_x, entry]
            side = spot & 1
            lanes = pl.ds(pl.multiple_of((spot >> 1) * LANES, LANES), LANES)
            base = pl.multiple_of((cell_y * ENTRIES + entry) * BLOCK, BLOCK)
            pair = wide_ref[pl.ds(base + cell_x, HALF, stride=2), :]
            mask = jnp.where(side == 0, low, high)
            for parity, value in ((side, pair), (1 - side, pltpu.roll(pair, BLOCK, 1))):
                rows = pl.ds(pl.multiple_of(parity * CELLS * HALF + cell * HALF, HALF), HALF)
                stores.append(((rows, lanes), out_ref[rows, lanes] + value.astype(jnp.bfloat16) * mask))
        for where, value in stores:
            out_ref[where] = value
        return carry

    lax.fori_loop(0, ENTRIES, place, 0, unroll=5)


def build(blocks, cols, count):
    rows = blocks.reshape(SIDE, SIDE, ENTRIES, HALF, LANES).transpose(0, 2, 3, 1, 4).reshape(BLOCK_ROWS, LANES)
    return pl.pallas_call(
        build_kernel,
        out_shape=jax.ShapeDtypeStruct((ROWS, DEPTH + LANES), jnp.bfloat16),
        in_specs=[smem(), vmem()],
        out_specs=vmem(),
        scratch_shapes=[pltpu.VMEM(rows.shape, jnp.float32)],
        compiler_params=pltpu.CompilerParams(vmem_limit_bytes=16 * 2**20),
        cost_estimate=pl.CostEstimate(flops=10_000_000, bytes_accessed=4_000_000, transcendentals=0),
    )(spots_of(cols, count), rows)


def product(mat_ref, part_refs, turn_ref):
    total = None
    for index, part_ref in enumerate(part_refs):
        term = jnp.dot(mat_ref[:, index * ROWS : (index + 1) * ROWS], part_ref[:ROWS], preferred_element_type=jnp.float32)
        total = term if total is None else total + term
    for cell in range(CELLS):
        for parity in range(2):
            first = parity * CELLS * HALF + cell * HALF
            turn_ref[pl.ds(cell * BLOCK + parity, HALF, stride=2), :] = total[first : first + HALF]
    return turn_ref[...]


def write_note(note, sums):
    row = lax.broadcasted_iota(jnp.int32, (NOTE, SLAB), 0)
    rest = jnp.broadcast_to(sums, (NOTE, SLAB))
    rows = jnp.zeros((NOTE, SLAB), jnp.float32)
    for index in range(3):
        term = rest.astype(jnp.bfloat16).astype(jnp.float32)
        rows = jnp.where(row == index, term, rows)
        rest = rest - term
    note[ROWS:, :] = rows.astype(jnp.bfloat16)


def read_notes(part_refs):
    notes = [jnp.sum(ref[ROWS:, :].astype(jnp.float32), axis=0, keepdims=True) for ref in part_refs]
    return notes[0] + notes[1] + notes[2] + notes[3]


def root_kernel(mat_ref, *refs):
    *part_refs, out_ref, turn_ref = refs
    own = part_refs[0][:ROWS].astype(jnp.float32)
    out_ref[...] = (own + product(mat_ref, part_refs, turn_ref)).astype(jnp.bfloat16)


def hamilton_kernel(mat_ref, *refs):
    *part_refs, out_ref, turn_ref = refs
    out_ref[...] = product(mat_ref, part_refs, turn_ref).astype(jnp.bfloat16)


def power_kernel(mat_ref, slab_ref, *refs):
    *part_refs, out_ref, power_ref, turn_ref = refs
    power = part_refs[0][...].astype(jnp.float32) + product(mat_ref, part_refs, turn_ref)
    slab = slab_ref[...].astype(jnp.float32)
    power_ref[...] = power
    out_ref[:ROWS] = power.astype(jnp.bfloat16)
    lane = lax.broadcasted_iota(jnp.int32, (1, SLAB), 1)
    write_note(out_ref, jnp.where(lane < SLAB // 2, jnp.sum(power * power), jnp.sum(slab * slab)))


def root_sums_kernel(mat_ref, *refs):
    *part_refs, out_ref, sums_ref, turn_ref = refs
    sums_ref[...] = jnp.broadcast_to(read_notes([part_refs[part] for part in (0, 1, 3, 4)]), sums_ref.shape)
    root_kernel(mat_ref, *part_refs, out_ref, turn_ref)


def hamilton_sums_kernel(mat_ref, term_ref, other_ref, *refs):
    *part_refs, out_ref, turn_ref = refs
    out_ref[:ROWS] = product(mat_ref, part_refs, turn_ref).astype(jnp.bfloat16)
    write_note(out_ref, term_ref[:1] + other_ref[:1])


def last_kernel(mat_ref, slab_ref, power_ref, *refs):
    *part_refs, one_ref, two_ref, turn_ref = refs
    sums = read_notes([part_refs[part] for part in (0, 2, 6, 8)])
    ratio = jnp.sqrt(sums[:, :1] / (sums[:, SLAB // 2 : SLAB // 2 + 1] + 1e-06))
    image = part_refs[0][:ROWS].astype(jnp.float32) + product(mat_ref, part_refs, turn_ref)
    one_ref[...] = (power_ref[...] / ratio).astype(jnp.bfloat16)
    two_ref[...] = (2.0 * (image / ratio) / ratio - slab_ref[...].astype(jnp.float32)).astype(jnp.bfloat16)


def apply(kernel, outs, *operands):
    return pl.pallas_call(
        kernel,
        out_shape=outs,
        in_specs=[vmem()] * len(operands),
        out_specs=jax.tree.map(lambda _: vmem(), outs),
        scratch_shapes=[pltpu.VMEM((ROWS, SLAB), jnp.float32)],
        compiler_params=pltpu.CompilerParams(vmem_limit_bytes=16 * 2**20),
        cost_estimate=pl.CostEstimate(flops=2 * ROWS * DEPTH * SLAB, bytes_accessed=2_000_000, transcendentals=0),
    )(*operands)


def same(index, count):
    return index


def near(index, count):
    return index ^ 1


def cross(index, count):
    return (index + 1 if index % 2 else index - 1) % count


def swap(value, row_map, col_map):
    rows, cols = lax.axis_size("row"), lax.axis_size("col")
    pairs = [(r * cols + c, row_map(r, rows) * cols + col_map(c, cols)) for r in range(rows) for c in range(cols)]
    return lax.ppermute(value, ("row", "col"), pairs)


def surround(field):
    across_same = swap(field, same, cross)
    near_y = swap(field, near, same)
    far_y = swap(field, cross, same)
    beside = swap(field, same, near)
    beside_near = swap(near_y, same, near)
    beside_far = swap(far_y, same, near)
    across_far = swap(across_same, cross, same)
    across_near = swap(across_same, near, same)
    return [field, near_y, far_y, beside, beside_near, beside_far, across_same, across_near, across_far]


def shifted(sums, axis, step):
    count = lax.axis_size(axis)
    return lax.ppermute(sums, axis, [(i, (i + step) % count) for i in range(count)])


def body(x_slab, h_blocks, h_cols, h_count, z_blocks, z_cols, z_count):
    z_mat = build(z_blocks, z_cols, z_count)
    h_mat = build(h_blocks, h_cols, h_count)
    flat = jax.ShapeDtypeStruct((ROWS, SLAB), jnp.bfloat16)
    wide = jax.ShapeDtypeStruct((ROWS, SLAB), jnp.float32)
    sums_shape = jax.ShapeDtypeStruct((8, SLAB), jnp.float32)
    noted = jax.ShapeDtypeStruct((ROWS + NOTE, SLAB), jnp.bfloat16)
    slab = x_slab.reshape(ROWS, SLAB)

    u_one = apply(root_kernel, flat, z_mat, *surround(slab))
    u_two = apply(hamilton_kernel, flat, h_mat, *surround(u_one))
    power, power_full = apply(power_kernel, (noted, wide), z_mat, slab, *surround(u_two))

    v_one, sums = apply(root_sums_kernel, (flat, sums_shape), z_mat, *surround(power))
    ring = sums + shifted(sums, "col", 4) + shifted(sums, "col", 8) + shifted(sums, "col", 12)
    other = shifted(ring, "row", 4)
    v_two = apply(hamilton_sums_kernel, noted, h_mat, ring, other, *surround(v_one))
    one, two = apply(last_kernel, (flat, flat), z_mat, slab, power_full, *surround(v_two))
    return one.reshape(x_slab.shape), two.reshape(x_slab.shape)


def solution(mesh):
    in_specs = (
        P("row", "col", None, None),
        P("row", "col", None, None),
        P("row", "col", None),
        P("row", "col"),
        P("row", "col", None, None),
        P("row", "col", None),
        P("row", "col"),
    )
    out_specs = (P("row", "col", None, None), P("row", "col", None, None))
    return jax.shard_map(body, mesh=mesh, in_specs=in_specs, out_specs=out_specs, check_vma=False)
```

```python
import jax
import jax.numpy as jnp
from jax import lax
from jax.experimental import pallas as pl
from jax.experimental.pallas import tpu as pltpu
from jax.sharding import PartitionSpec as P

REACH = 2
SIDE = 2
BLOCK = 64
SLAB = 128
ENTRIES = 25
LAT_Y = 16
LAT_X = 32
CELLS = SIDE * SIDE
HALF = BLOCK // 2
LANES = 2 * BLOCK
ROWS = CELLS * BLOCK
PARTS = 9
DEPTH = PARTS * ROWS
NOTE = 16
BLOCK_ROWS = CELLS * ENTRIES * HALF


def vmem():
    return pl.BlockSpec(memory_space=pltpu.VMEM)


def smem():
    return pl.BlockSpec(memory_space=pltpu.SMEM)


def role(step, is_odd):
    return jnp.where(step == 1, 0, jnp.where((step == 2) == (is_odd == 0), 1, 2))


def spots_of(cols, count):
    row, col = lax.axis_index("row"), lax.axis_index("col")
    cell_y = lax.broadcasted_iota(jnp.int32, cols.shape, 0)
    cell_x = lax.broadcasted_iota(jnp.int32, cols.shape, 1)
    win_y = (((cols >> LAT_X.bit_length() - 1) - row * SIDE - cell_y + REACH) & (LAT_Y - 1)) + cell_y
    win_x = (((cols & (LAT_X - 1)) - col * SIDE - cell_x + REACH) & (LAT_X - 1)) + cell_x
    part = role(win_x >> 1, col & 1) * 3 + role(win_y >> 1, row & 1)
    live = lax.broadcasted_iota(jnp.int32, cols.shape, 2) < count[:, :, None]
    return jnp.where(live, part * 2 + (win_y & 1), 2 * PARTS) * 2 + (win_x & 1)


def build_kernel(spots_ref, blocks_ref, out_ref, wide_ref):
    out_ref[...] = jnp.zeros_like(out_ref)
    wide_ref[...] = blocks_ref[...].astype(jnp.float32)
    lane_half = lax.broadcasted_iota(jnp.int32, (HALF, LANES), 1) // BLOCK
    low = (lane_half == 0).astype(jnp.float32).astype(jnp.bfloat16)
    high = (lane_half == 1).astype(jnp.float32).astype(jnp.bfloat16)

    def place(entry, carry):
        stores = []
        for cell in range(CELLS):
            cell_y, cell_x = divmod(cell, SIDE)
            spot = spots_ref[cell_y, cell_x, entry]
            side = spot & 1
            lanes = pl.ds(pl.multiple_of((spot >> 1) * LANES, LANES), LANES)
            base = pl.multiple_of((cell_y * ENTRIES + entry) * BLOCK, BLOCK)
            pair = wide_ref[pl.ds(base + cell_x, HALF, stride=2), :]
            mask = jnp.where(side == 0, low, high)
            for parity, value in ((side, pair), (1 - side, pltpu.roll(pair, BLOCK, 1))):
                rows = pl.ds(pl.multiple_of(parity * CELLS * HALF + cell * HALF, HALF), HALF)
                stores.append(((rows, lanes), out_ref[rows, lanes] + value.astype(jnp.bfloat16) * mask))
        for where, value in stores:
            out_ref[where] = value
        return carry

    lax.fori_loop(0, ENTRIES, place, 0, unroll=5)


def build(blocks, cols, count):
    rows = blocks.reshape(SIDE, SIDE, ENTRIES, HALF, LANES).transpose(0, 2, 3, 1, 4).reshape(BLOCK_ROWS, LANES)
    return pl.pallas_call(
        build_kernel,
        out_shape=jax.ShapeDtypeStruct((ROWS, DEPTH + LANES), jnp.bfloat16),
        in_specs=[smem(), vmem()],
        out_specs=vmem(),
        scratch_shapes=[pltpu.VMEM(rows.shape, jnp.float32)],
        compiler_params=pltpu.CompilerParams(vmem_limit_bytes=16 * 2**20),
        cost_estimate=pl.CostEstimate(flops=10_000_000, bytes_accessed=4_000_000, transcendentals=0),
    )(spots_of(cols, count), rows)


def product(mat_ref, part_refs, turn_ref):
    total = None
    for index, part_ref in enumerate(part_refs):
        term = jnp.dot(mat_ref[:, index * ROWS : (index + 1) * ROWS], part_ref[:ROWS], preferred_element_type=jnp.float32)
        total = term if total is None else total + term
    for cell in range(CELLS):
        for parity in range(2):
            first = parity * CELLS * HALF + cell * HALF
            turn_ref[pl.ds(cell * BLOCK + parity, HALF, stride=2), :] = total[first : first + HALF]
    return turn_ref[...]


def write_note(note, sums):
    row = lax.broadcasted_iota(jnp.int32, (NOTE, SLAB), 0)
    rest = jnp.broadcast_to(sums, (NOTE, SLAB))
    rows = jnp.zeros((NOTE, SLAB), jnp.float32)
    for index in range(3):
        term = rest.astype(jnp.bfloat16).astype(jnp.float32)
        rows = jnp.where(row == index, term, rows)
        rest = rest - term
    note[ROWS:, :] = rows.astype(jnp.bfloat16)


def read_notes(part_refs):
    notes = [jnp.sum(ref[ROWS:, :].astype(jnp.float32), axis=0, keepdims=True) for ref in part_refs]
    return notes[0] + notes[1] + notes[2] + notes[3]


def root_kernel(mat_ref, *refs):
    *part_refs, out_ref, turn_ref = refs
    own = part_refs[0][:ROWS].astype(jnp.float32)
    out_ref[...] = (own + product(mat_ref, part_refs, turn_ref)).astype(jnp.bfloat16)


def hamilton_kernel(mat_ref, *refs):
    *part_refs, out_ref, turn_ref = refs
    out_ref[...] = product(mat_ref, part_refs, turn_ref).astype(jnp.bfloat16)


def power_kernel(mat_ref, slab_ref, *refs):
    *part_refs, out_ref, power_ref, turn_ref = refs
    power = part_refs[0][...].astype(jnp.float32) + product(mat_ref, part_refs, turn_ref)
    slab = slab_ref[...].astype(jnp.float32)
    power_ref[...] = power
    out_ref[:ROWS] = power.astype(jnp.bfloat16)
    lane = lax.broadcasted_iota(jnp.int32, (1, SLAB), 1)
    write_note(out_ref, jnp.where(lane < SLAB // 2, jnp.sum(power * power), jnp.sum(slab * slab)))


def root_sums_kernel(mat_ref, *refs):
    *part_refs, out_ref, sums_ref, turn_ref = refs
    sums_ref[...] = jnp.broadcast_to(read_notes([part_refs[part] for part in (0, 1, 3, 4)]), sums_ref.shape)
    root_kernel(mat_ref, *part_refs, out_ref, turn_ref)


def hamilton_sums_kernel(mat_ref, term_ref, other_ref, *refs):
    *part_refs, out_ref, turn_ref = refs
    out_ref[:ROWS] = product(mat_ref, part_refs, turn_ref).astype(jnp.bfloat16)
    write_note(out_ref, term_ref[:1] + other_ref[:1])


def last_kernel(mat_ref, slab_ref, power_ref, *refs):
    *part_refs, one_ref, two_ref, turn_ref = refs
    sums = read_notes([part_refs[part] for part in (0, 2, 6, 8)])
    ratio = jnp.sqrt(sums[:, :1] / (sums[:, SLAB // 2 : SLAB // 2 + 1] + 1e-06))
    image = part_refs[0][:ROWS].astype(jnp.float32) + product(mat_ref, part_refs, turn_ref)
    one_ref[...] = (power_ref[...] / ratio).astype(jnp.bfloat16)
    two_ref[...] = (2.0 * (image / ratio) / ratio - slab_ref[...].astype(jnp.float32)).astype(jnp.bfloat16)


def apply(kernel, outs, *operands):
    return pl.pallas_call(
        kernel,
        out_shape=outs,
        in_specs=[vmem()] * len(operands),
        out_specs=jax.tree.map(lambda _: vmem(), outs),
        scratch_shapes=[pltpu.VMEM((ROWS, SLAB), jnp.float32)],
        compiler_params=pltpu.CompilerParams(vmem_limit_bytes=16 * 2**20),
        cost_estimate=pl.CostEstimate(flops=2 * ROWS * DEPTH * SLAB, bytes_accessed=2_000_000, transcendentals=0),
    )(*operands)


def same(index, count):
    return index


def near(index, count):
    return index ^ 1


def cross(index, count):
    return (index + 1 if index % 2 else index - 1) % count


def swap(value, row_map, col_map):
    rows, cols = lax.axis_size("row"), lax.axis_size("col")
    pairs = [(r * cols + c, row_map(r, rows) * cols + col_map(c, cols)) for r in range(rows) for c in range(cols)]
    return lax.ppermute(value, ("row", "col"), pairs)


def surround(field):
    across_same = swap(field, same, cross)
    near_y = swap(field, near, same)
    far_y = swap(field, cross, same)
    beside = swap(field, same, near)
    beside_near = swap(near_y, same, near)
    beside_far = swap(far_y, same, near)
    across_far = swap(field, cross, cross)
    across_near = swap(across_same, near, same)
    return [field, near_y, far_y, beside, beside_near, beside_far, across_same, across_near, across_far]


def shifted(sums, axis, step):
    count = lax.axis_size(axis)
    return lax.ppermute(sums, axis, [(i, (i + step) % count) for i in range(count)])


def body(x_slab, h_blocks, h_cols, h_count, z_blocks, z_cols, z_count):
    z_mat = build(z_blocks, z_cols, z_count)
    h_mat = build(h_blocks, h_cols, h_count)
    flat = jax.ShapeDtypeStruct((ROWS, SLAB), jnp.bfloat16)
    wide = jax.ShapeDtypeStruct((ROWS, SLAB), jnp.float32)
    sums_shape = jax.ShapeDtypeStruct((8, SLAB), jnp.float32)
    noted = jax.ShapeDtypeStruct((ROWS + NOTE, SLAB), jnp.bfloat16)
    slab = x_slab.reshape(ROWS, SLAB)

    u_one = apply(root_kernel, flat, z_mat, *surround(slab))
    u_two = apply(hamilton_kernel, flat, h_mat, *surround(u_one))
    power, power_full = apply(power_kernel, (noted, wide), z_mat, slab, *surround(u_two))

    v_one, sums = apply(root_sums_kernel, (flat, sums_shape), z_mat, *surround(power))
    ring = sums + shifted(sums, "col", 4) + shifted(sums, "col", 8) + shifted(sums, "col", 12)
    other = shifted(ring, "row", 4)
    v_two = apply(hamilton_sums_kernel, noted, h_mat, ring, other, *surround(v_one))
    one, two = apply(last_kernel, (flat, flat), z_mat, slab, power_full, *surround(v_two))
    return one.reshape(x_slab.shape), two.reshape(x_slab.shape)


def solution(mesh):
    in_specs = (
        P("row", "col", None, None),
        P("row", "col", None, None),
        P("row", "col", None),
        P("row", "col"),
        P("row", "col", None, None),
        P("row", "col", None),
        P("row", "col"),
    )
    out_specs = (P("row", "col", None, None), P("row", "col", None, None))
    return jax.shard_map(body, mesh=mesh, in_specs=in_specs, out_specs=out_specs, check_vma=False)
```

```python
import jax
import jax.numpy as jnp
from jax import lax
from jax.experimental import pallas as pl
from jax.experimental.pallas import tpu as pltpu
from jax.sharding import PartitionSpec as P

REACH = 2
SIDE = 2
BLOCK = 64
SLAB = 128
ENTRIES = 25
LAT_Y = 16
LAT_X = 32
CELLS = SIDE * SIDE
HALF = BLOCK // 2
LANES = 2 * BLOCK
ROWS = CELLS * BLOCK
PARTS = 9
DEPTH = PARTS * ROWS
NOTE = 16
EARLY = (0, 1, 2, 6)
LATE = (3, 4, 5, 7, 8)
BLOCK_ROWS = CELLS * ENTRIES * HALF


def vmem():
    return pl.BlockSpec(memory_space=pltpu.VMEM)


def smem():
    return pl.BlockSpec(memory_space=pltpu.SMEM)


def role(step, is_odd):
    return jnp.where(step == 1, 0, jnp.where((step == 2) == (is_odd == 0), 1, 2))


def spots_of(cols, count):
    row, col = lax.axis_index("row"), lax.axis_index("col")
    cell_y = lax.broadcasted_iota(jnp.int32, cols.shape, 0)
    cell_x = lax.broadcasted_iota(jnp.int32, cols.shape, 1)
    win_y = (((cols >> LAT_X.bit_length() - 1) - row * SIDE - cell_y + REACH) & (LAT_Y - 1)) + cell_y
    win_x = (((cols & (LAT_X - 1)) - col * SIDE - cell_x + REACH) & (LAT_X - 1)) + cell_x
    part = role(win_x >> 1, col & 1) * 3 + role(win_y >> 1, row & 1)
    live = lax.broadcasted_iota(jnp.int32, cols.shape, 2) < count[:, :, None]
    return jnp.where(live, part * 2 + (win_y & 1), 2 * PARTS) * 2 + (win_x & 1)


def build_kernel(spots_ref, blocks_ref, out_ref, wide_ref):
    out_ref[...] = jnp.zeros_like(out_ref)
    wide_ref[...] = blocks_ref[...].astype(jnp.float32)
    lane_half = lax.broadcasted_iota(jnp.int32, (HALF, LANES), 1) // BLOCK
    low = (lane_half == 0).astype(jnp.float32).astype(jnp.bfloat16)
    high = (lane_half == 1).astype(jnp.float32).astype(jnp.bfloat16)

    def place(entry, carry):
        stores = []
        for cell in range(CELLS):
            cell_y, cell_x = divmod(cell, SIDE)
            spot = spots_ref[cell_y, cell_x, entry]
            side = spot & 1
            lanes = pl.ds(pl.multiple_of((spot >> 1) * LANES, LANES), LANES)
            base = pl.multiple_of((cell_y * ENTRIES + entry) * BLOCK, BLOCK)
            pair = wide_ref[pl.ds(base + cell_x, HALF, stride=2), :]
            mask = jnp.where(side == 0, low, high)
            for parity, value in ((side, pair), (1 - side, pltpu.roll(pair, BLOCK, 1))):
                rows = pl.ds(pl.multiple_of(parity * CELLS * HALF + cell * HALF, HALF), HALF)
                stores.append(((rows, lanes), out_ref[rows, lanes] + value.astype(jnp.bfloat16) * mask))
        for where, value in stores:
            out_ref[where] = value
        return carry

    lax.fori_loop(0, ENTRIES, place, 0, unroll=5)


def build(blocks, cols, count):
    rows = blocks.reshape(SIDE, SIDE, ENTRIES, HALF, LANES).transpose(0, 2, 3, 1, 4).reshape(BLOCK_ROWS, LANES)
    return pl.pallas_call(
        build_kernel,
        out_shape=jax.ShapeDtypeStruct((ROWS, DEPTH + LANES), jnp.bfloat16),
        in_specs=[smem(), vmem()],
        out_specs=vmem(),
        scratch_shapes=[pltpu.VMEM(rows.shape, jnp.float32)],
        compiler_params=pltpu.CompilerParams(vmem_limit_bytes=16 * 2**20),
        cost_estimate=pl.CostEstimate(flops=10_000_000, bytes_accessed=4_000_000, transcendentals=0),
    )(spots_of(cols, count), rows)


def partial(mat_ref, part_refs, indices):
    total = None
    for index in indices:
        columns = mat_ref[:, index * ROWS : (index + 1) * ROWS]
        term = jnp.dot(columns, part_refs[index][:ROWS], preferred_element_type=jnp.float32)
        total = term if total is None else total + term
    return total


def early_kernel(mat_ref, *refs):
    *part_refs, total_ref = refs
    total_ref[...] = partial(mat_ref, dict(zip(EARLY, part_refs)), EARLY)


def product(mats, part_refs, turn_ref):
    mat_ref, early_ref = mats
    total = early_ref[...] + partial(mat_ref, part_refs, LATE)
    for cell in range(CELLS):
        for parity in range(2):
            first = parity * CELLS * HALF + cell * HALF
            turn_ref[pl.ds(cell * BLOCK + parity, HALF, stride=2), :] = total[first : first + HALF]
    return turn_ref[...]


def write_note(note, sums):
    row = lax.broadcasted_iota(jnp.int32, (NOTE, SLAB), 0)
    rest = jnp.broadcast_to(sums, (NOTE, SLAB))
    rows = jnp.zeros((NOTE, SLAB), jnp.float32)
    for index in range(3):
        term = rest.astype(jnp.bfloat16).astype(jnp.float32)
        rows = jnp.where(row == index, term, rows)
        rest = rest - term
    note[ROWS:, :] = rows.astype(jnp.bfloat16)


def read_notes(part_refs):
    notes = [jnp.sum(ref[ROWS:, :].astype(jnp.float32), axis=0, keepdims=True) for ref in part_refs]
    return notes[0] + notes[1] + notes[2] + notes[3]


def root_kernel(mat_ref, *refs):
    *part_refs, out_ref, turn_ref = refs
    own = part_refs[0][:ROWS].astype(jnp.float32)
    out_ref[...] = (own + product(mat_ref, part_refs, turn_ref)).astype(jnp.bfloat16)


def hamilton_kernel(mat_ref, *refs):
    *part_refs, out_ref, turn_ref = refs
    out_ref[...] = product(mat_ref, part_refs, turn_ref).astype(jnp.bfloat16)


def power_kernel(mat_ref, slab_ref, *refs):
    *part_refs, out_ref, power_ref, turn_ref = refs
    power = part_refs[0][...].astype(jnp.float32) + product(mat_ref, part_refs, turn_ref)
    slab = slab_ref[...].astype(jnp.float32)
    power_ref[...] = power
    out_ref[:ROWS] = power.astype(jnp.bfloat16)
    lane = lax.broadcasted_iota(jnp.int32, (1, SLAB), 1)
    write_note(out_ref, jnp.where(lane < SLAB // 2, jnp.sum(power * power), jnp.sum(slab * slab)))


def root_sums_kernel(mat_ref, *refs):
    *part_refs, out_ref, sums_ref, turn_ref = refs
    sums_ref[...] = jnp.broadcast_to(read_notes([part_refs[part] for part in (0, 1, 3, 4)]), sums_ref.shape)
    root_kernel(mat_ref, *part_refs, out_ref, turn_ref)


def hamilton_sums_kernel(mat_ref, term_ref, other_ref, *refs):
    *part_refs, out_ref, turn_ref = refs
    out_ref[:ROWS] = product(mat_ref, part_refs, turn_ref).astype(jnp.bfloat16)
    write_note(out_ref, term_ref[:1] + other_ref[:1])


def last_kernel(mat_ref, slab_ref, power_ref, *refs):
    *part_refs, one_ref, two_ref, turn_ref = refs
    sums = read_notes([part_refs[part] for part in (0, 2, 6, 8)])
    ratio = jnp.sqrt(sums[:, :1] / (sums[:, SLAB // 2 : SLAB // 2 + 1] + 1e-06))
    image = part_refs[0][:ROWS].astype(jnp.float32) + product(mat_ref, part_refs, turn_ref)
    one_ref[...] = (power_ref[...] / ratio).astype(jnp.bfloat16)
    two_ref[...] = (2.0 * (image / ratio) / ratio - slab_ref[...].astype(jnp.float32)).astype(jnp.bfloat16)


def call(kernel, outs, scratch, *operands):
    return pl.pallas_call(
        kernel,
        out_shape=outs,
        in_specs=[vmem()] * len(operands),
        out_specs=jax.tree.map(lambda _: vmem(), outs),
        scratch_shapes=scratch,
        compiler_params=pltpu.CompilerParams(vmem_limit_bytes=16 * 2**20),
        cost_estimate=pl.CostEstimate(flops=ROWS * DEPTH * SLAB, bytes_accessed=1_000_000, transcendentals=0),
    )(*operands)


def apply(kernel, outs, mat, *operands):
    parts = operands[-PARTS:]
    wide = jax.ShapeDtypeStruct((ROWS, SLAB), jnp.float32)
    early = call(early_kernel, wide, [], mat, *(parts[index] for index in EARLY))

    def late_kernel(mat_ref, early_ref, *refs):
        kernel((mat_ref, early_ref), *refs)

    return call(late_kernel, outs, [pltpu.VMEM((ROWS, SLAB), jnp.float32)], mat, early, *operands)


def same(index, count):
    return index


def near(index, count):
    return index ^ 1


def cross(index, count):
    return (index + 1 if index % 2 else index - 1) % count


def swap(value, row_map, col_map):
    rows, cols = lax.axis_size("row"), lax.axis_size("col")
    pairs = [(r * cols + c, row_map(r, rows) * cols + col_map(c, cols)) for r in range(rows) for c in range(cols)]
    return lax.ppermute(value, ("row", "col"), pairs)


def surround(field, together=True):
    across_same = swap(field, same, cross)
    near_y = swap(field, near, same)
    far_y = swap(field, cross, same)
    beside = swap(field, same, near)
    if together:
        beside, across_same = lax.optimization_barrier((beside, across_same))
    beside_near = swap(near_y, same, near)
    beside_far = swap(far_y, same, near)
    across_far = swap(field, cross, cross)
    across_near = swap(across_same, near, same)
    return [field, near_y, far_y, beside, beside_near, beside_far, across_same, across_near, across_far]


def shifted(sums, axis, step):
    count = lax.axis_size(axis)
    return lax.ppermute(sums, axis, [(i, (i + step) % count) for i in range(count)])


def body(x_slab, h_blocks, h_cols, h_count, z_blocks, z_cols, z_count):
    z_mat = build(z_blocks, z_cols, z_count)
    h_mat = build(h_blocks, h_cols, h_count)
    flat = jax.ShapeDtypeStruct((ROWS, SLAB), jnp.bfloat16)
    wide = jax.ShapeDtypeStruct((ROWS, SLAB), jnp.float32)
    sums_shape = jax.ShapeDtypeStruct((8, SLAB), jnp.float32)
    noted = jax.ShapeDtypeStruct((ROWS + NOTE, SLAB), jnp.bfloat16)
    slab = x_slab.reshape(ROWS, SLAB)

    u_one = apply(root_kernel, flat, z_mat, *surround(slab))
    u_two = apply(hamilton_kernel, flat, h_mat, *surround(u_one))
    power, power_full = apply(power_kernel, (noted, wide), z_mat, slab, *surround(u_two))

    v_one, sums = apply(root_sums_kernel, (flat, sums_shape), z_mat, *surround(power))
    ring = sums + shifted(sums, "col", 4) + shifted(sums, "col", 8) + shifted(sums, "col", 12)
    other = shifted(ring, "row", 4)
    v_two = apply(hamilton_sums_kernel, noted, h_mat, ring, other, *surround(v_one, together=False))
    one, two = apply(last_kernel, (flat, flat), z_mat, slab, power_full, *surround(v_two))
    return one.reshape(x_slab.shape), two.reshape(x_slab.shape)


def solution(mesh):
    in_specs = (
        P("row", "col", None, None),
        P("row", "col", None, None),
        P("row", "col", None),
        P("row", "col"),
        P("row", "col", None, None),
        P("row", "col", None),
        P("row", "col"),
    )
    out_specs = (P("row", "col", None, None), P("row", "col", None, None))
    return jax.shard_map(body, mesh=mesh, in_specs=in_specs, out_specs=out_specs, check_vma=False)
```

```python
import jax
import jax.numpy as jnp
from jax import lax
from jax.experimental import pallas as pl
from jax.experimental.pallas import tpu as pltpu
from jax.sharding import PartitionSpec as P

REACH = 2
SIDE = 2
BLOCK = 64
SLAB = 128
ENTRIES = 25
LAT_Y = 16
LAT_X = 32
CELLS = SIDE * SIDE
HALF = BLOCK // 2
LANES = 2 * BLOCK
ROWS = CELLS * BLOCK
PARTS = 9
DEPTH = PARTS * ROWS
NOTE = 16
EARLY = (0, 1, 2, 6)
LATE = (3, 4, 5, 7, 8)
BLOCK_ROWS = CELLS * ENTRIES * HALF


def vmem():
    return pl.BlockSpec(memory_space=pltpu.VMEM)


def smem():
    return pl.BlockSpec(memory_space=pltpu.SMEM)


def role(step, is_odd):
    return jnp.where(step == 1, 0, jnp.where((step == 2) == (is_odd == 0), 1, 2))


def spots_of(cols, count):
    row, col = lax.axis_index("row"), lax.axis_index("col")
    cell_y = lax.broadcasted_iota(jnp.int32, cols.shape, 0)
    cell_x = lax.broadcasted_iota(jnp.int32, cols.shape, 1)
    win_y = (((cols >> LAT_X.bit_length() - 1) - row * SIDE - cell_y + REACH) & (LAT_Y - 1)) + cell_y
    win_x = (((cols & (LAT_X - 1)) - col * SIDE - cell_x + REACH) & (LAT_X - 1)) + cell_x
    part = role(win_x >> 1, col & 1) * 3 + role(win_y >> 1, row & 1)
    live = lax.broadcasted_iota(jnp.int32, cols.shape, 2) < count[:, :, None]
    return jnp.where(live, part * 2 + (win_y & 1), 2 * PARTS) * 2 + (win_x & 1)


def build_kernel(spots_ref, blocks_ref, out_ref, wide_ref):
    out_ref[...] = jnp.zeros_like(out_ref)
    wide_ref[...] = blocks_ref[...].astype(jnp.float32)
    lane_half = lax.broadcasted_iota(jnp.int32, (HALF, LANES), 1) // BLOCK
    low = (lane_half == 0).astype(jnp.float32).astype(jnp.bfloat16)
    high = (lane_half == 1).astype(jnp.float32).astype(jnp.bfloat16)

    def place(entry, carry):
        stores = []
        for cell in range(CELLS):
            cell_y, cell_x = divmod(cell, SIDE)
            spot = spots_ref[cell_y, cell_x, entry]
            side = spot & 1
            lanes = pl.ds(pl.multiple_of((spot >> 1) * LANES, LANES), LANES)
            base = pl.multiple_of((cell_y * ENTRIES + entry) * BLOCK, BLOCK)
            pair = wide_ref[pl.ds(base + cell_x, HALF, stride=2), :]
            mask = jnp.where(side == 0, low, high)
            for parity, value in ((side, pair), (1 - side, pltpu.roll(pair, BLOCK, 1))):
                rows = pl.ds(pl.multiple_of(parity * CELLS * HALF + cell * HALF, HALF), HALF)
                stores.append(((rows, lanes), out_ref[rows, lanes] + value.astype(jnp.bfloat16) * mask))
        for where, value in stores:
            out_ref[where] = value
        return carry

    lax.fori_loop(0, ENTRIES, place, 0, unroll=5)


def build(blocks, cols, count):
    rows = blocks.reshape(SIDE, SIDE, ENTRIES, HALF, LANES).transpose(0, 2, 3, 1, 4).reshape(BLOCK_ROWS, LANES)
    return pl.pallas_call(
        build_kernel,
        out_shape=jax.ShapeDtypeStruct((ROWS, DEPTH + LANES), jnp.bfloat16),
        in_specs=[smem(), vmem()],
        out_specs=vmem(),
        scratch_shapes=[pltpu.VMEM(rows.shape, jnp.float32)],
        compiler_params=pltpu.CompilerParams(vmem_limit_bytes=16 * 2**20),
        cost_estimate=pl.CostEstimate(flops=10_000_000, bytes_accessed=4_000_000, transcendentals=0),
    )(spots_of(cols, count), rows)


def partial(mat_ref, part_refs, indices):
    total = None
    for index in indices:
        columns = mat_ref[:, index * ROWS : (index + 1) * ROWS]
        term = jnp.dot(columns, part_refs[index][:ROWS], preferred_element_type=jnp.float32)
        total = term if total is None else total + term
    return total


def early_kernel(mat_ref, *refs):
    *part_refs, total_ref = refs
    total_ref[...] = partial(mat_ref, dict(zip(EARLY, part_refs)), EARLY)


def product(mats, part_refs, turn_ref):
    mat_ref, early_ref = mats
    total = early_ref[...] + partial(mat_ref, part_refs, LATE)
    for cell in range(CELLS):
        for parity in range(2):
            first = parity * CELLS * HALF + cell * HALF
            turn_ref[pl.ds(cell * BLOCK + parity, HALF, stride=2), :] = total[first : first + HALF]
    return turn_ref[...]


def write_note(note, sums):
    row = lax.broadcasted_iota(jnp.int32, (NOTE, SLAB), 0)
    rest = jnp.broadcast_to(sums, (NOTE, SLAB))
    rows = jnp.zeros((NOTE, SLAB), jnp.float32)
    for index in range(3):
        term = rest.astype(jnp.bfloat16).astype(jnp.float32)
        rows = jnp.where(row == index, term, rows)
        rest = rest - term
    note[ROWS:, :] = rows.astype(jnp.bfloat16)


def read_notes(part_refs):
    notes = [jnp.sum(ref[ROWS:, :].astype(jnp.float32), axis=0, keepdims=True) for ref in part_refs]
    return notes[0] + notes[1] + notes[2] + notes[3]


def root_kernel(mat_ref, *refs):
    *part_refs, out_ref, turn_ref = refs
    own = part_refs[0][:ROWS].astype(jnp.float32)
    out_ref[...] = (own + product(mat_ref, part_refs, turn_ref)).astype(jnp.bfloat16)


def hamilton_kernel(mat_ref, *refs):
    *part_refs, out_ref, turn_ref = refs
    out_ref[...] = product(mat_ref, part_refs, turn_ref).astype(jnp.bfloat16)


def power_kernel(mat_ref, slab_ref, *refs):
    *part_refs, out_ref, power_ref, turn_ref = refs
    power = part_refs[0][...].astype(jnp.float32) + product(mat_ref, part_refs, turn_ref)
    slab = slab_ref[...].astype(jnp.float32)
    power_ref[...] = power
    out_ref[:ROWS] = power.astype(jnp.bfloat16)
    lane = lax.broadcasted_iota(jnp.int32, (1, SLAB), 1)
    write_note(out_ref, jnp.where(lane < SLAB // 2, jnp.sum(power * power), jnp.sum(slab * slab)))


def root_sums_kernel(mat_ref, *refs):
    *part_refs, out_ref, sums_ref, turn_ref = refs
    sums_ref[...] = jnp.broadcast_to(read_notes([part_refs[part] for part in (0, 1, 3, 4)]), sums_ref.shape)
    root_kernel(mat_ref, *part_refs, out_ref, turn_ref)


def hamilton_sums_kernel(mat_ref, term_ref, other_ref, *refs):
    *part_refs, out_ref, turn_ref = refs
    out_ref[:ROWS] = product(mat_ref, part_refs, turn_ref).astype(jnp.bfloat16)
    write_note(out_ref, term_ref[:1] + other_ref[:1])


def last_kernel(mat_ref, slab_ref, power_ref, *refs):
    *part_refs, one_ref, two_ref, turn_ref = refs
    sums = read_notes([part_refs[part] for part in (0, 2, 6, 8)])
    ratio = jnp.sqrt(sums[:, :1] / (sums[:, SLAB // 2 : SLAB // 2 + 1] + 1e-06))
    image = part_refs[0][:ROWS].astype(jnp.float32) + product(mat_ref, part_refs, turn_ref)
    inverse = 1.0 / ratio
    one_ref[...] = (power_ref[...] * inverse).astype(jnp.bfloat16)
    two_ref[...] = ((image * inverse) * (2.0 * inverse) - slab_ref[...].astype(jnp.float32)).astype(jnp.bfloat16)


def call(kernel, outs, scratch, *operands):
    return pl.pallas_call(
        kernel,
        out_shape=outs,
        in_specs=[vmem()] * len(operands),
        out_specs=jax.tree.map(lambda _: vmem(), outs),
        scratch_shapes=scratch,
        compiler_params=pltpu.CompilerParams(vmem_limit_bytes=16 * 2**20),
        cost_estimate=pl.CostEstimate(flops=ROWS * DEPTH * SLAB, bytes_accessed=1_000_000, transcendentals=0),
    )(*operands)


def apply(kernel, outs, mat, *operands):
    parts = operands[-PARTS:]
    wide = jax.ShapeDtypeStruct((ROWS, SLAB), jnp.float32)
    early = call(early_kernel, wide, [], mat, *(parts[index] for index in EARLY))

    def late_kernel(mat_ref, early_ref, *refs):
        kernel((mat_ref, early_ref), *refs)

    return call(late_kernel, outs, [pltpu.VMEM((ROWS, SLAB), jnp.float32)], mat, early, *operands)


def same(index, count):
    return index


def near(index, count):
    return index ^ 1


def cross(index, count):
    return (index + 1 if index % 2 else index - 1) % count


def swap(value, row_map, col_map):
    rows, cols = lax.axis_size("row"), lax.axis_size("col")
    pairs = [(r * cols + c, row_map(r, rows) * cols + col_map(c, cols)) for r in range(rows) for c in range(cols)]
    return lax.ppermute(value, ("row", "col"), pairs)


def surround(field, together=True):
    across_same = swap(field, same, cross)
    near_y = swap(field, near, same)
    far_y = swap(field, cross, same)
    beside = swap(field, same, near)
    if together:
        beside, across_same = lax.optimization_barrier((beside, across_same))
    beside_near = swap(near_y, same, near)
    beside_far = swap(far_y, same, near)
    across_far = swap(field, cross, cross)
    across_near = swap(across_same, near, same)
    return [field, near_y, far_y, beside, beside_near, beside_far, across_same, across_near, across_far]


def shifted(sums, axis, step):
    count = lax.axis_size(axis)
    return lax.ppermute(sums, axis, [(i, (i + step) % count) for i in range(count)])


def body(x_slab, h_blocks, h_cols, h_count, z_blocks, z_cols, z_count):
    z_mat = build(z_blocks, z_cols, z_count)
    h_mat = build(h_blocks, h_cols, h_count)
    flat = jax.ShapeDtypeStruct((ROWS, SLAB), jnp.bfloat16)
    wide = jax.ShapeDtypeStruct((ROWS, SLAB), jnp.float32)
    sums_shape = jax.ShapeDtypeStruct((8, SLAB), jnp.float32)
    noted = jax.ShapeDtypeStruct((ROWS + NOTE, SLAB), jnp.bfloat16)
    slab = x_slab.reshape(ROWS, SLAB)

    u_one = apply(root_kernel, flat, z_mat, *surround(slab))
    u_two = apply(hamilton_kernel, flat, h_mat, *surround(u_one))
    power, power_full = apply(power_kernel, (noted, wide), z_mat, slab, *surround(u_two))

    v_one, sums = apply(root_sums_kernel, (flat, sums_shape), z_mat, *surround(power))
    ring = sums + shifted(sums, "col", 4) + shifted(sums, "col", 8) + shifted(sums, "col", 12)
    other = shifted(ring, "row", 4)
    v_two = apply(hamilton_sums_kernel, noted, h_mat, ring, other, *surround(v_one, together=False))
    one, two = apply(last_kernel, (flat, flat), z_mat, slab, power_full, *surround(v_two))
    return one.reshape(x_slab.shape), two.reshape(x_slab.shape)


def solution(mesh):
    in_specs = (
        P("row", "col", None, None),
        P("row", "col", None, None),
        P("row", "col", None),
        P("row", "col"),
        P("row", "col", None, None),
        P("row", "col", None),
        P("row", "col"),
    )
    out_specs = (P("row", "col", None, None), P("row", "col", None, None))
    return jax.shard_map(body, mesh=mesh, in_specs=in_specs, out_specs=out_specs, check_vma=False)
```
